256 devices in a mesh: energy: 8 (over y, x_hi), slab: 32 (over z, x_lo, core).
Axes of the slice: x: 4 (x_hi: 2, x_lo: 2; x = x_hi * 2 + x_lo), y: 4, z: 8, core: 2. Of those that a mesh axis runs over, the one named last changes fastest.
Arguments:
- lower_block: float32 [8, 32, 2, 256, 256], P('energy', 'slab'), may hold values from -1 to 1
- pivot_inverse: float32 [8, 32, 2, 256, 256], P('energy', 'slab'), may hold values from -1 to 1
- upper_block: float32 [8, 32, 2, 256, 256], P('energy', 'slab'), may hold values from -1 to 1
- coulomb: float32 [8, 32, 2, 256, 128], P('energy', 'slab'), may hold values from -2.5 to 2.5
- greens: bfloat16 [32, 32, 2, 256, 128], P('energy', 'slab'), may hold values from -6 to 6
- offsets: int32 [8], replicated, may hold values from -4 to 4, as said below
Outputs:
- screened: bfloat16 [8, 32, 2, 256, 128], P('energy', 'slab')
- self_energy: bfloat16 [32, 32, 2, 256, 128], P('energy', 'slab')
The draws below stay inside these ranges and needn't reach their ends.
Inputs may be any that keep to these rules, and one draw needn't show every extreme that they name: `offsets`: both -4 and 4 occur.
All inputs are finite; a program needn't handle non-finite values.
Results may differ from the reference program's by a relative error of at most 0.0049.
Values may be sent and summed in bfloat16 or wider, within the bound.
A program may use at most 128 MiB of HBM per device.

```python
import math
import jax
import jax.numpy as jnp
from jax import lax

B = 256
R = 128
SEGMENT_TOTAL = 32
NE = 32
SPECTRAL_POINTS = 8
HALO = 4


def coupling_blocks(key, slow_share, blend_share):
    sampler_seeds = jax.random.split(key, 7)
    slow_mask = jax.random.uniform(sampler_seeds[0], (SPECTRAL_POINTS, 1, B)) < slow_share
    fast_keep = jnp.exp(-jax.random.uniform(sampler_seeds[1], (SPECTRAL_POINTS, 1, B), minval=0.7, maxval=2.0))
    variation = jnp.exp(jax.random.uniform(sampler_seeds[2], (SPECTRAL_POINTS, SEGMENT_TOTAL, B), minval=-0.7, maxval=0.7))
    slow_keep = jnp.exp(-0.2 * variation / SEGMENT_TOTAL)
    kept_fraction = jnp.where(slow_mask, slow_keep, fast_keep ** variation)
    batch_span = jax.random.uniform(sampler_seeds[3], (SPECTRAL_POINTS, SEGMENT_TOTAL, 1)) < 2.0 / SEGMENT_TOTAL
    truncation_scale = jax.random.uniform(sampler_seeds[4], (SPECTRAL_POINTS, SEGMENT_TOTAL, 1), minval=0.5, maxval=0.8)
    kept_fraction = kept_fraction * jnp.where(batch_span, truncation_scale, 1.0) * math.sqrt(1.0 - blend_share * blend_share)
    phases = jax.random.uniform(sampler_seeds[5], (SPECTRAL_POINTS, SEGMENT_TOTAL, B), minval=-math.pi, maxval=math.pi)
    identity = jnp.eye(B, dtype=jnp.float32)
    real_diag = (kept_fraction * jnp.cos(phases))[..., None, :] * identity
    imag_diag = (kept_fraction * jnp.sin(phases))[..., None, :] * identity
    spread_part = jnp.clip(jax.random.normal(sampler_seeds[6], (SPECTRAL_POINTS, SEGMENT_TOTAL, 2, B, B)), -5.0, 5.0) * blend_share / math.sqrt(2.0 * B)
    return jnp.clip(jnp.stack([real_diag, imag_diag], axis=2) + spread_part, -1.0, 1.0)


def draw_lower_block(key, part):
    key = jax.random.fold_in(key, 11)
    return coupling_blocks(key, 0.5, 0.2)


def draw_upper_block(key, part):
    key = jax.random.fold_in(key, 13)
    return coupling_blocks(key, 0.5, 0.2)


def draw_pivot_inverse(key, part):
    key = jax.random.fold_in(key, 17)
    sampler_seeds = jax.random.split(key, 3)
    gains = jax.random.uniform(sampler_seeds[0], (SPECTRAL_POINTS, SEGMENT_TOTAL, B), minval=0.5, maxval=1.5)
    phases = jax.random.uniform(sampler_seeds[1], (SPECTRAL_POINTS, SEGMENT_TOTAL, B), minval=-math.pi, maxval=math.pi)
    identity = jnp.eye(B, dtype=jnp.float32)
    real_diag = (gains * jnp.cos(phases))[..., None, :] * identity
    imag_diag = (gains * jnp.sin(phases))[..., None, :] * identity
    spread_part = jnp.clip(jax.random.normal(sampler_seeds[2], (SPECTRAL_POINTS, SEGMENT_TOTAL, 2, B, B)), -5.0, 5.0) * 0.3 / math.sqrt(2.0 * B)
    blocks = (jnp.stack([real_diag, imag_diag], axis=2) + spread_part) * 2.0 / math.sqrt(SEGMENT_TOTAL)
    return jnp.clip(blocks, -1.0, 1.0)


def draw_offsets(key, part):
    key = jax.random.fold_in(key, 19)
    sampler_seeds = jax.random.split(key, 2)
    values = jax.random.randint(sampler_seeds[0], (SPECTRAL_POINTS,), -HALO, HALO + 1, dtype=jnp.int32)
    order = jax.random.permutation(sampler_seeds[1], SPECTRAL_POINTS)
    values = values.at[order[0]].set(-HALO)
    values = values.at[order[1]].set(HALO)
    return values.astype(jnp.int32)


def shard_levels(key, extent, cuts, least, top_value):
    factor_of, own = 1.0, jax.random.fold_in(key, 6)
    for dim, blocks in cuts:
        draws = jnp.exp(jax.random.uniform(jax.random.fold_in(own, dim), (blocks,), jnp.float32, least / len(cuts), top_value / len(cuts)))
        factor_of = factor_of * jnp.repeat(draws, extent[dim] // blocks).reshape([-1 if axis == dim else 1 for axis in range(len(extent))])
    return factor_of


def centred(own_key, extent, width, reach, shards=(), kind=jnp.bfloat16):
    drawn = jax.random.normal(own_key, extent, jnp.float32) * width
    if len(shards) > 0:
        drawn = shard_levels(own_key, extent, shards, -0.22, 0.18) * drawn
    return jnp.clip(drawn, min=-reach, max=reach).astype(kind)


def setup_inputs(seed: int = 0) -> dict:
    key_list = jax.random.split(jax.random.key(seed), 7)
    return {
        "lower_block": draw_lower_block(jax.random.fold_in(key_list[6], 71), 0),
        "pivot_inverse": draw_pivot_inverse(jax.random.fold_in(key_list[6], 71), 0),
        "upper_block": draw_upper_block(jax.random.fold_in(key_list[6], 71), 0),
        "coulomb": centred(key_list[3], (SPECTRAL_POINTS, SEGMENT_TOTAL, 2, B, R), (SEGMENT_TOTAL ** -0.5), 2.5, ((0, 8), (1, 32)), jnp.float32),
        "greens": centred(key_list[4], (NE, SEGMENT_TOTAL, 2, B, R), 1.0, 6.0, ((0, 8), (1, 32))),
        "offsets": draw_offsets(jax.random.fold_in(key_list[6], 71), 0),
    }


def matmul_batch(former, latter):
    return jnp.einsum("fik,fkj->fij", former, latter, precision=lax.Precision.HIGHEST)


def complex_product(former, latter):
    real_part = matmul_batch(former[:, 0], latter[:, 0]) - matmul_batch(former[:, 1], latter[:, 1])
    imag_part = matmul_batch(former[:, 0], latter[:, 1]) + matmul_batch(former[:, 1], latter[:, 0])
    return jnp.stack([real_part, imag_part], axis=1)


def entry_product(green_part, screen_part):
    green_re = green_part[..., 0, :, :]
    green_im = green_part[..., 1, :, :]
    screen_re = screen_part[..., 0, :, :]
    screen_im = screen_part[..., 1, :, :]
    return jnp.stack([green_re * screen_re - green_im * screen_im, green_re * screen_im + green_im * screen_re], axis=-3)


def chain_step(carried, inputs):
    couple, source = inputs
    value = source - complex_product(couple, carried)
    return value, value


def reference(lower_block, pivot_inverse, upper_block, coulomb, greens, offsets):
    lower_steps = jnp.moveaxis(lower_block, 1, 0)
    pivot_steps = jnp.moveaxis(pivot_inverse, 1, 0)
    upper_steps = jnp.moveaxis(upper_block, 1, 0)
    source_steps = jnp.moveaxis(coulomb, 1, 0)
    start_value = jnp.zeros(source_steps.shape[1:], jnp.float32)
    final_value, forward_values = lax.scan(chain_step, start_value, (lower_steps, source_steps))
    flat_pivot = pivot_steps.reshape((-1,) + pivot_steps.shape[2:])
    flat_values = forward_values.reshape((-1,) + forward_values.shape[2:])
    projected = complex_product(flat_pivot, flat_values).reshape(forward_values.shape)
    final_back, backward_values = lax.scan(chain_step, start_value, (upper_steps, projected), reverse=True)
    screened = jnp.moveaxis(backward_values, 0, 1).astype(jnp.bfloat16)

    def add_term(item, running):
        shifted = jnp.roll(greens, offsets[item], axis=0).astype(jnp.float32)
        screen_term = lax.dynamic_index_in_dim(screened, item, 0, keepdims=False).astype(jnp.float32)
        return running + entry_product(shifted, screen_term)

    self_energy = lax.fori_loop(0, SPECTRAL_POINTS, add_term, jnp.zeros(greens.shape, jnp.float32))
    return screened, self_energy.astype(jnp.bfloat16)
```

```python
import functools

import jax
import jax.numpy as jnp
from jax import lax
from jax.experimental import pallas as pl
from jax.experimental.pallas import tpu as pltpu
from jax.sharding import PartitionSpec as P

MESH = pl.DeviceIdType.MESH
LANES = 128
BF16 = jnp.bfloat16
F32 = jnp.float32


def dot(a, b):
    return jnp.dot(a, b, preferred_element_type=F32)


def put_stack(ref, part, value):
    n = value.shape[0]
    hi = value.astype(BF16)
    ref[part, 0:n] = hi
    ref[part, n : 2 * n] = (value - hi.astype(F32)).astype(BF16)


def matrix_product(a, b):
    n = a.shape[2]

    def real_product(i, j):
        both = dot(a[i], b[j, 0:n])
        return both[0:n] + both[n : 2 * n] + dot(a[i, 0:n], b[j, n : 2 * n])

    return (
        real_product(0, 0) - real_product(1, 1),
        real_product(0, 1) + real_product(1, 0),
    )


def lane_of(n):
    return lax.broadcasted_iota(jnp.int32, (n, LANES), 1)


def times_i(w):
    f = w.astype(F32)
    group = lane_of(w.shape[0]) // 32
    return jnp.where(group % 2 == 0, -pltpu.roll(f, 96, 1), pltpu.roll(f, 32, 1)).astype(BF16)


def apply(a, w):
    n = a.shape[2]
    r = dot(a[0], w) + dot(a[1], times_i(w))
    return r[0:n] + r[n : 2 * n]


def fold(s):
    return s + pltpu.roll(s, 64, 1)


def to_chunk(v):
    hi = v.astype(BF16).astype(F32)
    return jnp.where(lane_of(v.shape[0]) < 64, hi, v - hi).astype(BF16)


def wide(w):
    return w.astype(F32)


def split_columns(re, im, j):
    lane = lane_of(re.shape[0])
    re = pltpu.roll(re, (LANES - 32 * j) % LANES, 1) if j else re
    im = pltpu.roll(im, (LANES - 32 * j + 32) % LANES, 1)
    pair = jnp.where(lane < 32, re, im)
    return to_chunk(jnp.where(lane < 64, pair, pltpu.roll(pair, 64, 1)))


def chain_kernel(
    nz,
    lower,
    pivot,
    upper,
    coulomb,
    greens,
    screened,
    before,
    after,
    load,
    cin,
    mst,
    A1,
    D1,
    E1,
    b1,
    e1,
    bstage,
    estage,
    A2,
    D2,
    E2,
    b2,
    e2,
    Ag,
    Dg,
    Eg,
    tmp,
    vin,
    vout,
    win,
    wout,
    beta,
    vr,
    zin,
    zout,
    result,
    load_sem,
    s_sem,
    r_sem,
    out_sem,
):
    e = lax.axis_index("energy")
    s = lax.axis_index("slab")
    ne = lax.axis_size("energy")
    ns = 4 * nz
    c = lax.rem(s, 2)
    xi = lax.rem(s // 2, 2)
    z = s // 4
    sib = (e, s + 1 - 2 * c)
    xp = (e, s + 2 - 4 * xi)
    zup = (e, lax.rem(s + 4, ns))
    zdn = (e, lax.rem(s + ns - 4, ns))
    eup = (lax.rem(e + 1, ne), s)
    edn = (lax.rem(e + ne - 1, ne), s)
    counter = [0]
    sends = []

    def remote(src, dst, to, k=None):
        if k is None:
            k = counter[0]
            counter[0] += 1
        return pltpu.make_async_remote_copy(
            src_ref=src,
            dst_ref=dst,
            send_sem=s_sem.at[k],
            recv_sem=r_sem.at[k],
            device_id=to,
            device_id_type=MESH,
        )

    def go(src, dst, to):
        copy = remote(src, dst, to)
        copy.start()
        sends.append(copy)
        return copy

    loads = []
    for k, (src, dst) in enumerate(
        [
            (lower.at[0, 0], load.at[0]),
            (coulomb.at[0, 0], cin),
            (pivot.at[0, 0], load.at[1]),
            (upper.at[0, 0], load.at[2]),
        ]
    ):
        copy = pltpu.make_async_copy(src, dst, load_sem.at[k])
        copy.start()
        loads.append(copy)

    barrier = pltpu.get_barrier_semaphore()
    for to in (sib, xp, zup, zdn, eup, edn):
        pl.semaphore_signal(barrier, inc=1, device_id=to, device_id_type=MESH)

    loads[0].wait()
    for part in range(2):
        put_stack(A1.at[c], part, -load[0, part])
    pl.semaphore_wait(barrier, 6)
    a1 = go(A1.at[c], A1.at[c], sib)
    loads[1].wait()
    chunks = [split_columns(cin[0], cin[1], j) for j in range(4)]
    for j in range(2):
        b1[c, j] = jnp.where(c == 0, chunks[j], chunks[2 + j])
        bstage[j] = jnp.where(c == 0, chunks[2 + j], chunks[j])
    bb1 = go(bstage, b1.at[c], sib)
    loads[3].wait()
    for part in range(2):
        put_stack(D1.at[c], part, -load[2, part])
    d1 = go(D1.at[c], D1.at[c], sib)
    bb1.wait_recv()
    a1.wait_recv()
    for j in range(2):
        b2[xi, j] = to_chunk(fold(apply(A1[1], b1[0, j]) + wide(b1[1, j])))
    bb2 = go(b2.at[xi], b2.at[xi], xp)
    re, im = matrix_product(A1.at[1], A1.at[0])
    put_stack(A2.at[xi], 0, re)
    put_stack(A2.at[xi], 1, im)
    a2 = go(A2.at[xi, c], A2.at[xi, c], xp)
    loads[2].wait()
    for part in range(2):
        put_stack(mst, part, load[1, part])
    re, im = matrix_product(mst, A1.at[c])
    put_stack(E1.at[c], 0, re)
    put_stack(E1.at[c], 1, im)
    ee1 = go(E1.at[c], E1.at[c], sib)
    for j in range(2):
        e1[c, j] = to_chunk(fold(apply(mst, b1[c, j])))
        estage[j] = to_chunk(fold(apply(mst, bstage[j])))
    e1c = go(estage, e1.at[c], sib)
    d1.wait_recv()
    re, im = matrix_product(D1.at[0], D1.at[1])
    put_stack(D2.at[xi], 0, re)
    put_stack(D2.at[xi], 1, im)
    ee1.wait_recv()
    re, im = matrix_product(E1.at[1], A1.at[0])
    put_stack(tmp, 0, re)
    put_stack(tmp, 1, im)
    re, im = matrix_product(D1.at[0], tmp)
    for part, value in ((0, re), (1, im)):
        n = value.shape[0]
        put_stack(E2.at[xi], part, value + wide(E1[0, part, 0:n]) + wide(E1[0, part, n : 2 * n]))
    e1c.wait_recv()
    for j in range(2):
        inner = to_chunk(fold(apply(E1[1], b1[0, j]) + wide(e1[1, j])))
        e2[xi, j] = to_chunk(fold(apply(D1[0], inner) + wide(e1[0, j])))
    bb2.wait_recv()
    a2.wait_recv()
    a2f = go(A2.at[1 - xi, c], A2.at[1 - xi, c], sib)
    ee2 = go(E2.at[xi, c], E2.at[xi, c], xp)
    e2c = go(e2.at[xi], e2.at[xi], xp)
    d2 = go(D2.at[xi, c], D2.at[xi, c], xp)
    a2f.wait_recv()
    bg = vout
    for j in range(2):
        bg[0, j] = to_chunk(fold(apply(A2[1], b2[0, j]) + wide(b2[1, j])))

    def backward_maps():
        ee2.wait_recv()
        ee2f.start()
        d2.wait_recv()
        d2f.start()
        e2c.wait_recv()
        ee2f.wait_recv()
        re, im = matrix_product(E2.at[1], A2.at[0])
        put_stack(tmp, 0, re)
        put_stack(tmp, 1, im)
        d2f.wait_recv()
        re, im = matrix_product(D2.at[0], tmp)
        for part, value in ((0, re), (1, im)):
            n = value.shape[0]
            put_stack(Eg, part, value + wide(E2[0, part, 0:n]) + wide(E2[0, part, n : 2 * n]))
        re, im = matrix_product(D2.at[0], D2.at[1])
        put_stack(Dg, 0, re)
        put_stack(Dg, 1, im)

    ee2f = remote(E2.at[1 - xi, c], E2.at[1 - xi, c], sib)
    d2f = remote(D2.at[1 - xi, c], D2.at[1 - xi, c], sib)
    fwd = [remote(vout.at[1, j], vin.at[j], zup) for j in range(2)]
    first = [remote(vout.at[0, j], vin.at[j], zup, counter[0] - 2 + j) for j in range(2)]
    back = [remote(wout.at[j], win.at[j], zdn) for j in range(2)]

    @pl.when(z == 0)
    def _():
        for j in range(2):
            first[j].start()
            vin[j] = jnp.zeros_like(vin[j])

    re, im = matrix_product(A2.at[1], A2.at[0])
    put_stack(Ag, 0, re)
    put_stack(Ag, 1, im)
    halo_up = go(greens, before, eup)
    halo_dn = go(greens, after, edn)

    @pl.when(z >= nz // 2)
    def _():
        backward_maps()

    @pl.when(z > 0)
    def _():
        for j in range(2):
            fwd[j].wait_recv()

            @pl.when(z < nz - 1)
            def _():
                vout[1, j] = to_chunk(fold(apply(Ag, vin[j]) + wide(bg[0, j])))
                fwd[j].start()

    @pl.when(z < nz // 2)
    def _():
        backward_maps()

    for j in range(2):
        inner = to_chunk(fold(apply(E2[1], b2[0, j]) + wide(e2[1, j])))
        eg = fold(apply(D2[0], inner) + wide(e2[0, j]))
        beta[j] = eg + fold(apply(Eg, vin[j]))

        @pl.when(z == nz - 1)
        def _():
            wout[j] = to_chunk(beta[j])
            back[j].start()
            win[j] = jnp.zeros_like(win[j])

    for j in range(2):
        vr[j] = to_chunk(fold(apply(A2[0], vin[j]) + wide(b2[0, j])))

    @pl.when(z < nz - 1)
    def _():
        for j in range(2):
            back[j].wait_recv()

            @pl.when(z > 0)
            def _():
                wout[j] = to_chunk(fold(apply(Dg, win[j])) + beta[j])
                back[j].start()

    lane = lane_of(vin.shape[1])
    left, right = [], []
    for j in range(2):
        vc = jnp.where(xi == 0, vin[j], vr[j])
        wl = to_chunk(fold(apply(D2[1], win[j]) + apply(E2[1], vr[j]) + wide(e2[1, j])))
        wc = jnp.where(xi == 0, wl, win[j])
        left.append(fold(apply(D2[xi], wc) + apply(E2[xi], vc) + wide(e2[xi, j])))
        vs = to_chunk(fold(apply(A1[0], vc) + wide(b1[0, j])))
        right.append(fold(apply(D1[1], wc) + apply(E1[1], vs) + wide(e1[1, j])))

    def gather_columns(parts):
        first32 = jnp.where(lane < 32, parts[0], pltpu.roll(parts[1], 32, 1))
        last32 = jnp.where(lane < 96, pltpu.roll(parts[0], 32, 1), parts[1])
        return jnp.where(lane < 64, first32, last32)

    left, right = gather_columns(left), gather_columns(right)
    zout[...] = jnp.where(c == 0, right, left).astype(BF16)
    zc = go(zout, zin, sib)
    own = jnp.where(c == 0, left, right)
    zc.wait_recv()
    other = zin[...].astype(F32)
    z0 = jnp.where(c == 0, own, other)
    z1 = jnp.where(c == 0, other, own)
    result[0] = jnp.where(lane < 64, z0, pltpu.roll(z1, 64, 1)).astype(BF16)
    result[1] = jnp.where(lane < 64, pltpu.roll(z0, 64, 1), z1).astype(BF16)
    out = pltpu.make_async_copy(result, screened.at[0, 0], out_sem)
    out.start()
    out.wait()
    for copy in sends:
        copy.wait_send()
    ee2f.wait_send()
    d2f.wait_send()
    for j in range(2):

        @pl.when(z < nz - 1)
        def _():
            fwd[j].wait_send()

        @pl.when(z > 0)
        def _():
            back[j].wait_send()

    halo_up.wait_recv()
    halo_dn.wait_recv()


def chain(nz, lower, pivot, upper, coulomb, greens):
    n = lower.shape[-1]
    stack = (2, 2 * n, n)
    chunk = (n, LANES)
    any_space = pl.BlockSpec(memory_space=pl.ANY)
    return pl.pallas_call(
        functools.partial(chain_kernel, nz),
        out_shape=[
            jax.ShapeDtypeStruct(coulomb.shape, BF16),
            jax.ShapeDtypeStruct(greens.shape, BF16),
            jax.ShapeDtypeStruct(greens.shape, BF16),
        ],
        in_specs=[any_space] * 5,
        out_specs=[any_space] * 3,
        scratch_shapes=[
            pltpu.VMEM((3, 2, n, n), F32),
            pltpu.VMEM((2, n, LANES), F32),
            pltpu.VMEM(stack, BF16),
            pltpu.VMEM((2,) + stack, BF16),
            pltpu.VMEM((2,) + stack, BF16),
            pltpu.VMEM((2,) + stack, BF16),
            pltpu.VMEM((2, 2) + chunk, BF16),
            pltpu.VMEM((2, 2) + chunk, BF16),
            pltpu.VMEM((2,) + chunk, BF16),
            pltpu.VMEM((2,) + chunk, BF16),
            pltpu.VMEM((2,) + stack, BF16),
            pltpu.VMEM((2,) + stack, BF16),
            pltpu.VMEM((2,) + stack, BF16),
            pltpu.VMEM((2, 2) + chunk, BF16),
            pltpu.VMEM((2, 2) + chunk, BF16),
            pltpu.VMEM(stack, BF16),
            pltpu.VMEM(stack, BF16),
            pltpu.VMEM(stack, BF16),
            pltpu.VMEM(stack, BF16),
            pltpu.VMEM((2,) + chunk, BF16),
            pltpu.VMEM((2, 2) + chunk, BF16),
            pltpu.VMEM((2,) + chunk, BF16),
            pltpu.VMEM((2,) + chunk, BF16),
            pltpu.VMEM((2,) + chunk, F32),
            pltpu.VMEM((2,) + chunk, BF16),
            pltpu.VMEM(chunk, BF16),
            pltpu.VMEM(chunk, BF16),
            pltpu.VMEM((2,) + chunk, BF16),
            pltpu.SemaphoreType.DMA((4,)),
            pltpu.SemaphoreType.DMA((32,)),
            pltpu.SemaphoreType.DMA((32,)),
            pltpu.SemaphoreType.DMA,
        ],
        compiler_params=pltpu.CompilerParams(
            collective_id=0, has_side_effects=True, vmem_limit_bytes=48 * 2**20
        ),
        name="chain",
    )(lower, pivot, upper, coulomb, greens)


def gather_kernel(
    offsets, screened, greens, before, after, out, port, ext, acc, load_sem, s_sem, r_sem
):
    e = lax.axis_index("energy")
    s = lax.axis_index("slab")
    ne = lax.axis_size("energy")
    rows = greens.shape[0]
    across = e + 1 - 2 * lax.rem(e, 2)
    up, down = lax.rem(e + 2, ne), lax.rem(e + ne - 2, ne)

    loads = []
    for k, (src, dst) in enumerate(
        [
            (screened.at[0, 0], port.at[e]),
            (greens.at[:, 0], ext.at[pl.ds(rows, rows)]),
            (before.at[:, 0], ext.at[pl.ds(0, rows)]),
            (after.at[:, 0], ext.at[pl.ds(2 * rows, rows)]),
        ]
    ):
        copy = pltpu.make_async_copy(src, dst, load_sem.at[k])
        copy.start()
        loads.append(copy)
    barrier = pltpu.get_barrier_semaphore()
    for to in (across, up, down):
        pl.semaphore_signal(barrier, inc=1, device_id=(to, s), device_id_type=MESH)
    pl.semaphore_wait(barrier, 3)
    sends = []

    def go(ref, to):
        k = len(sends)
        copy = pltpu.make_async_remote_copy(
            src_ref=ref,
            dst_ref=ref,
            send_sem=s_sem.at[k],
            recv_sem=r_sem.at[k],
            device_id=(to, s),
            device_id_type=MESH,
        )
        copy.start()
        sends.append(copy)
        return copy

    def across_of(i):
        return i + 1 - 2 * lax.rem(i, 2)

    loads[0].wait()
    t1 = go(port.at[e], across)
    t2 = go(port.at[e], up)
    t3 = go(port.at[e], down)
    for copy in loads[1:]:
        copy.wait()

    def add(group, start):
        n = port.shape[2]
        step = 16

        def tile(t, _):
            at = pl.ds(pl.multiple_of(t * step, step), step)
            w = [(port[f, 0, at].astype(F32), port[f, 1, at].astype(F32)) for f in group]
            for j in range(rows):
                if start:
                    re = im = jnp.zeros((step, LANES), F32)
                else:
                    re, im = acc[j, 0, at], acc[j, 1, at]
                for f, (wr, wi) in zip(group, w):
                    at_energy = rows - offsets[f] + j
                    gr = ext[at_energy, 0, at].astype(F32)
                    gi = ext[at_energy, 1, at].astype(F32)
                    re += gr * wr - gi * wi
                    im += gr * wi + gi * wr
                acc[j, 0, at], acc[j, 1, at] = re, im
            return 0

        lax.fori_loop(0, n // step, tile, 0)

    t1.wait_recv()
    t4 = go(port.at[across], up)
    t5 = go(port.at[across], down)
    t2.wait_recv()
    t6 = go(port.at[down, 0], up)
    t3.wait_recv()
    t7 = go(port.at[up, 1], down)
    add([e, across, down, up], True)
    t4.wait_recv()
    t8 = go(port.at[across_of(down), 0], up)
    t5.wait_recv()
    t9 = go(port.at[across_of(up), 1], down)
    opposite = lax.rem(e + 4, ne)
    t6.wait_recv()
    t7.wait_recv()
    t8.wait_recv()
    t9.wait_recv()
    add([across_of(down), across_of(up), opposite, across_of(opposite)], False)
    for j in range(rows):
        for part in range(2):
            out[j, 0, part] = acc[j, part].astype(BF16)
    for copy in sends:
        copy.wait_send()


def gather(ne, offsets, screened, greens, before, after):
    n = screened.shape[-2]
    rows = greens.shape[0]
    any_space = pl.BlockSpec(memory_space=pl.ANY)
    return pl.pallas_call(
        gather_kernel,
        out_shape=jax.ShapeDtypeStruct(greens.shape, BF16),
        in_specs=[pl.BlockSpec(memory_space=pltpu.SMEM)] + [any_space] * 4,
        out_specs=pl.BlockSpec(memory_space=pltpu.VMEM),
        scratch_shapes=[
            pltpu.VMEM((ne, 2, n, LANES), BF16),
            pltpu.VMEM((3 * rows, 2, n, LANES), BF16),
            pltpu.VMEM((rows, 2, n, LANES), F32),
            pltpu.SemaphoreType.DMA((4,)),
            pltpu.SemaphoreType.DMA((9,)),
            pltpu.SemaphoreType.DMA((9,)),
        ],
        compiler_params=pltpu.CompilerParams(
            collective_id=1, has_side_effects=True, vmem_limit_bytes=48 * 2**20
        ),
        name="gather",
    )(offsets, screened, greens, before, after)


def solution(mesh):
    nz = mesh.shape["slab"] // 4
    ne = mesh.shape["energy"]

    def shards(lower_block, pivot_inverse, upper_block, coulomb, greens, offsets):
        screened, before, after = chain(
            nz, lower_block, pivot_inverse, upper_block, coulomb, greens
        )
        return screened, gather(ne, offsets, screened, greens, before, after)

    block = P("energy", "slab", None, None, None)
    return jax.shard_map(
        shards,
        mesh=mesh,
        in_specs=(block,) * 5 + (P(),),
        out_specs=(block, block),
        check_vma=False,
    )
```

```python
import functools
import types

import jax
import jax.numpy as jnp
from jax import lax
from jax.experimental import pallas as pl
from jax.experimental.pallas import tpu as pltpu
from jax.sharding import PartitionSpec as P

MESH = pl.DeviceIdType.MESH
LANES = 128
BF16 = jnp.bfloat16
F32 = jnp.float32


def dot(a, b):
    return jnp.dot(a, b, preferred_element_type=F32)


def put_stack(ref, part, value):
    n = value.shape[0]
    hi = value.astype(BF16)
    ref[part, 0:n] = hi
    ref[part, n : 2 * n] = (value - hi.astype(F32)).astype(BF16)


def matrix_product(a, b):
    n = a.shape[2]

    def real_product(i, j):
        both = dot(a[i], b[j, 0:n])
        return both[0:n] + both[n : 2 * n] + dot(a[i, 0:n], b[j, n : 2 * n])

    return (
        real_product(0, 0) - real_product(1, 1),
        real_product(0, 1) + real_product(1, 0),
    )


def lane_of(n):
    return lax.broadcasted_iota(jnp.int32, (n, LANES), 1)


def times_i(w):
    f = w.astype(F32)
    group = lane_of(w.shape[0]) // 32
    return jnp.where(group % 2 == 0, -pltpu.roll(f, 96, 1), pltpu.roll(f, 32, 1)).astype(BF16)


def apply(a, w):
    n = a.shape[2]
    r = dot(a[0], w) + dot(a[1], times_i(w))
    return r[0:n] + r[n : 2 * n]


def apply_both(a, w0, w1):
    n = a.shape[2]
    w = jnp.concatenate([w0, w1], axis=1)
    iw = jnp.concatenate([times_i(w0), times_i(w1)], axis=1)
    r = dot(a[0], w) + dot(a[1], iw)
    r = r[0:n] + r[n : 2 * n]
    return r[:, 0:LANES], r[:, LANES : 2 * LANES]


def fold(s):
    return s + pltpu.roll(s, 64, 1)


def to_chunk(v):
    hi = v.astype(BF16).astype(F32)
    return jnp.where(lane_of(v.shape[0]) < 64, hi, v - hi).astype(BF16)


def wide(w):
    return w.astype(F32)


def split_columns(re, im, j):
    lane = lane_of(re.shape[0])
    re = pltpu.roll(re, (LANES - 32 * j) % LANES, 1) if j else re
    im = pltpu.roll(im, (LANES - 32 * j + 32) % LANES, 1)
    pair = jnp.where(lane < 32, re, im)
    return to_chunk(jnp.where(lane < 64, pair, pltpu.roll(pair, 64, 1)))


def put_product(ref, a, b):
    re, im = matrix_product(a, b)
    put_stack(ref, 0, re)
    put_stack(ref, 1, im)


def put_sum(ref, value, stack):
    for part in range(2):
        n = value[part].shape[0]
        put_stack(ref, part, value[part] + wide(stack[part, 0:n]) + wide(stack[part, n : 2 * n]))


def affine_both(a, w, b):
    s = apply_both(a, w[0], w[1])
    return [fold(s[j] + wide(b[j])) for j in range(2)]


def pack_columns(v0, v1):
    lane = lane_of(v0.shape[0])
    low = jnp.where(lane < 32, v0, pltpu.roll(v1, 32, 1))
    high = jnp.where(lane < 96, pltpu.roll(v0, 32, 1), v1)
    return jnp.where(lane < 64, low, high)


def unpack_halves(z0, z1):
    lane = lane_of(z0.shape[0])
    z0, z1 = z0.astype(F32), z1.astype(F32)
    re = jnp.where(lane < 64, z0, pltpu.roll(z1, 64, 1))
    im = jnp.where(lane < 64, pltpu.roll(z0, 64, 1), z1)
    return re, im


def kernel(nz, names, *refs):
    g = types.SimpleNamespace(**dict(zip(names, refs)))
    A1, D1, E1, b1, e1 = g.A1, g.D1, g.E1, g.b1, g.e1
    A2, D2, E2, b2, e2 = g.A2, g.D2, g.E2, g.b2, g.e2
    A3, D3, E3, b3, e3 = g.A3, g.D3, g.E3, g.b3, g.e3
    tmp, vin, vout, win, wout, port, ext = g.tmp, g.vin, g.vout, g.win, g.wout, g.port, g.ext

    e = lax.axis_index("energy")
    s = lax.axis_index("slab")
    ne = lax.axis_size("energy")
    ns = 4 * nz
    no = nz // 2
    rows = g.greens.shape[0]
    c = lax.rem(s, 2)
    xi = lax.rem(s // 2, 2)
    z = s // 4
    m = lax.rem(z, 2)
    o = z // 2
    h = lax.rem(e, 2)
    low = o < no // 2
    s_sib = s + 1 - 2 * c
    sib = (e, s_sib)
    xp = (e, s + 2 - 4 * xi)
    zup1, zup2 = (e, lax.rem(s + 4, ns)), (e, lax.rem(s + 8, ns))
    zdn1, zdn2 = (e, lax.rem(s + ns - 4, ns)), (e, lax.rem(s + ns - 8, ns))

    def across_of(i):
        return i + 1 - 2 * lax.rem(i, 2)

    across = across_of(e)
    yup, ydn = lax.rem(e + 2, ne), lax.rem(e + ne - 2, ne)
    peers = [(i, t) for i in (across, yup, ydn) for t in (s, s_sib)]

    send_ids, recv_ids = {}, {}
    sends = []

    def remote(name, src, dst, to, recv=None):
        k = send_ids.setdefault(name, len(send_ids))
        if isinstance(recv, tuple):
            base = recv_ids.setdefault(recv[0] + "0", len(recv_ids))
            recv_ids.setdefault(recv[0] + "1", len(recv_ids))
            r = base + recv[1]
        else:
            r = recv_ids.setdefault(recv or name, len(recv_ids))
        return pltpu.make_async_remote_copy(
            src_ref=src,
            dst_ref=dst,
            send_sem=g.s_sem.at[k],
            recv_sem=g.r_sem.at[r],
            device_id=to,
            device_id_type=MESH,
        )

    def go(*args):
        remote(*args).start()
        sends.append(args)

    def arrived(name, ref):
        remote("none", ref, ref, sib, name).wait_recv()

    def sent(name, src, dst, to):
        remote(name, src, dst, to, "none").wait_send()

    loads = []
    for k, (src, dst) in enumerate(
        [
            (g.lower.at[0, 0], g.load.at[0]),
            (g.coulomb.at[0, 0], g.cin),
            (g.upper.at[0, 0], g.load.at[2]),
            (g.pivot.at[0, 0], g.load.at[1]),
            (g.greens.at[:, 0], ext.at[pl.ds(rows, rows)]),
        ]
    ):
        copy = pltpu.make_async_copy(src, dst, g.load_sem.at[k])
        copy.start()
        loads.append(copy)

    barrier = pltpu.get_barrier_semaphore()
    partners = [sib, xp, zup1, zdn1, zup2, zdn2] + peers
    for to in partners:
        pl.semaphore_signal(barrier, inc=1, device_id=to, device_id_type=MESH)

    loads[0].wait()
    for part in range(2):
        put_stack(A1.at[c], part, -g.load[0, part])
    pl.semaphore_wait(barrier, len(partners))
    go("a1", A1.at[c], A1.at[c], sib)
    loads[1].wait()
    chunks = [split_columns(g.cin[0], g.cin[1], j) for j in range(4)]
    for j in range(2):
        g.bstage[j] = jnp.where(c == 0, chunks[2 + j], chunks[j])
    go("b1", g.bstage, b1.at[c], sib)
    for j in range(2):
        b1[c, j] = jnp.where(c == 0, chunks[j], chunks[2 + j])
    loads[2].wait()
    for part in range(2):
        put_stack(D1.at[c], part, -g.load[2, part])
    go("d1", D1.at[c], D1.at[c], sib)
    arrived("b1", b1.at[1 - c])
    arrived("a1", A1.at[1 - c])
    v = affine_both(A1.at[1], b1[0], b1[1])
    for j in range(2):
        b2[xi, j] = to_chunk(v[j])
    go("b2", b2.at[xi], b2.at[xi], xp)
    put_product(A2.at[xi], A1.at[1], A1.at[0])
    go("a2", A2.at[xi, c], A2.at[xi, c], xp, ("a2", c))
    loads[3].wait()
    for part in range(2):
        put_stack(g.mst, part, g.load[1, part])
    put_product(E1.at[c], g.mst, A1.at[c])
    go("e1m", E1.at[c], E1.at[c], sib)
    t = apply_both(g.mst, g.bstage[0], g.bstage[1])
    for j in range(2):
        g.estage[j] = to_chunk(fold(t[j]))
    go("e1", g.estage, e1.at[c], sib)
    t = apply_both(g.mst, b1[c, 0], b1[c, 1])
    for j in range(2):
        e1[c, j] = to_chunk(fold(t[j]))
    arrived("d1", D1.at[1 - c])
    arrived("e1m", E1.at[1 - c])
    put_product(tmp, E1.at[1], A1.at[0])
    put_sum(E2.at[xi], matrix_product(D1.at[0], tmp), E1.at[0])
    go("e2m", E2.at[xi, c], E2.at[xi, c], xp, ("e2m", c))
    put_product(D2.at[xi], D1.at[0], D1.at[1])
    go("d2", D2.at[xi, c], D2.at[xi, c], xp, ("d2", c))
    arrived("e1", e1.at[1 - c])

    def merged_e(D, E, ev, bv):
        inner = affine_both(E.at[1], bv[0], ev[1])
        inner = [to_chunk(v) for v in inner]
        return affine_both(D.at[0], inner, ev[0])

    v = merged_e(D1, E1, e1, b1)
    for j in range(2):
        e2[xi, j] = to_chunk(v[j])
    go("e2", e2.at[xi], e2.at[xi], xp)

    def half_arrived(name, ref):
        remote("none", ref.at[c], ref.at[c], sib, (name, c)).wait_recv()
        remote(name + "f", ref.at[c], ref.at[c], sib, (name + "f", c)).start()

    def other_half(name, ref):
        remote("none", ref.at[1 - c], ref.at[1 - c], sib, (name + "f", 1 - c)).wait_recv()

    arrived("b2", b2.at[1 - xi])
    half_arrived("a2", A2.at[1 - xi])
    other_half("a2", A2.at[1 - xi])
    v = affine_both(A2.at[1], b2[0], b2[1])
    for j in range(2):
        b3[m, j] = to_chunk(v[j])

    @pl.when(m == 0)
    def _():
        remote("b3", b3.at[0], b3.at[0], zup1).start()

    put_product(A3.at[m], A2.at[1], A2.at[0])

    @pl.when(m == 0)
    def _():
        remote("a3", A3.at[0, c], A3.at[0, c], zup1, ("a3", c)).start()

    def dir_start(name, ref, to):
        remote(name, ref, ref, to, (name, c)).start()

    def halo_pair():
        mine = ext.at[pl.ds(rows, rows)]
        theirs = ext.at[pl.ds(2 * rows * (1 - h), rows)]
        there = ext.at[pl.ds(2 * rows * h, rows)]
        return mine, theirs, there

    def quad_backward():
        half_arrived("e2m", E2.at[1 - xi])
        half_arrived("d2", D2.at[1 - xi])
        arrived("e2", e2.at[1 - xi])
        other_half("e2m", E2.at[1 - xi])
        put_product(tmp, E2.at[1], A2.at[0])
        other_half("d2", D2.at[1 - xi])
        put_sum(E3.at[m], matrix_product(D2.at[0], tmp), E2.at[0])

        @pl.when(m == 1)
        def _():
            dir_start("e3m", E3.at[1, c], zdn1)

        put_product(D3.at[m], D2.at[0], D2.at[1])

        @pl.when(m == 1)
        def _():
            dir_start("d3", D3.at[1, c], zdn1)

        v = merged_e(D2, E2, e2, b2)
        for j in range(2):
            e3[m, j] = to_chunk(v[j])

        @pl.when(m == 1)
        def _():
            remote("e3", e3.at[1], e3.at[1], zdn1).start()

        mine, theirs, there = halo_pair()
        loads[4].wait()
        remote("halo1", mine, there, (across, s)).start()

    def far(src, j):
        return remote("far%d" % j, src, vin.at[j], zup2, "v%d" % j)

    def near(src, j):
        return remote("near%d" % j, src, vin.at[j], zup1, "v%d" % j)

    @pl.when(o == 0)
    def _():
        vin[...] = jnp.zeros_like(vin)

    @pl.when(m == 1)
    def _():
        arrived("b3", b3.at[0])
        v = affine_both(A3.at[1], b3[0], b3[1])
        for j in range(2):
            vout[j] = to_chunk(v[j])

        @pl.when(o == 0)
        def _():
            for j in range(2):
                far(vout.at[j], j).start()

        remote("none", A3.at[0, c], A3.at[0, c], sib, ("a3", c)).wait_recv()
        remote("a3f", A3.at[0, c], A3.at[0, c], sib, ("a3f", c)).start()
        remote("none", A3.at[0, 1 - c], A3.at[0, 1 - c], sib, ("a3f", 1 - c)).wait_recv()

        @pl.when(o == 0)
        def _():
            for j in range(2):
                far(vout.at[j], j).wait_send()
                near(vout.at[j], j).start()

        @pl.when(o > 0)
        def _():
            put_product(g.Ao, A3.at[1], A3.at[0])

    @pl.when((m == 0) | jnp.logical_not(low))
    def _():
        quad_backward()

    @pl.when((m == 1) & (o > 0))
    def _():
        for j in range(2):
            arrived("v%d" % j, vin.at[j])

            @pl.when(o < no - 1)
            def _():
                vout[j] = to_chunk(fold(apply(g.Ao, vin[j]) + wide(vout[j])))

            @pl.when(o < no - 2)
            def _():
                far(vout.at[j], j).start()

            @pl.when(o == no - 2)
            def _():
                near(vout.at[j], j).start()

        @pl.when(o < no - 2)
        def _():
            for j in range(2):
                far(vout.at[j], j).wait_send()
                near(vout.at[j], j).start()

        @pl.when(o == no - 2)
        def _():
            for j in range(2):
                near(vout.at[j], j).wait_send()
                far(vout.at[j], j).start()

    @pl.when((m == 1) & low)
    def _():
        quad_backward()

    def wfar(j):
        return remote("wfar%d" % j, wout.at[j], win.at[j], zdn2, "w%d" % j)

    def wnear(j):
        return remote("wnear%d" % j, wout.at[j], win.at[j], zdn1, "w%d" % j)

    @pl.when(m == 0)
    def _():
        for name, ref in (("e3m", E3), ("d3", D3)):
            remote("none", ref.at[1, c], ref.at[1, c], sib, (name, c)).wait_recv()
            remote(name + "f", ref.at[1, c], ref.at[1, c], sib, (name + "f", c)).start()
        for name, ref in (("e3m", E3), ("d3", D3)):
            remote("none", ref.at[1, 1 - c], ref.at[1, 1 - c], sib, (name + "f", 1 - c)).wait_recv()
        put_product(tmp, E3.at[1], A3.at[0])
        put_sum(g.Eo, matrix_product(D3.at[0], tmp), E3.at[0])
        arrived("e3", e3.at[1])
        v = merged_e(D3, E3, e3, b3)
        for j in range(2):
            g.beta[j] = v[j]

        @pl.when(o > 0)
        def _():
            for j in range(2):
                arrived("v%d" % j, vin.at[j])
                g.beta[j] = g.beta[j] + fold(apply(g.Eo, vin[j]))

                @pl.when(o == no - 1)
                def _():
                    wout[j] = to_chunk(g.beta[j])
                    wfar(j).start()

        @pl.when(o == no - 1)
        def _():
            for j in range(2):
                wfar(j).wait_send()
                wnear(j).start()

        put_product(g.Do, D3.at[0], D3.at[1])

    @pl.when(o == no - 1)
    def _():
        win[...] = jnp.zeros_like(win)

    def both(ref):
        return [ref[0], ref[1]]

    vr3 = [to_chunk(v) for v in affine_both(A3.at[0], both(vin), b3[0])]
    vq = [jnp.where(m == 0, vin[j], vr3[j]) for j in range(2)]
    vr2 = [to_chunk(v) for v in affine_both(A2.at[0], vq, b2[0])]
    vc = [jnp.where(xi == 0, vq[j], vr2[j]) for j in range(2)]
    vs = [to_chunk(v) for v in affine_both(A1.at[0], vc, b1[0])]
    wq = [to_chunk(v) for v in affine_both(E3.at[1], vr3, e3[1])]
    wq = [jnp.where(m == 0, w, jnp.zeros_like(w)) for w in wq]
    t = apply_both(D2.at[1], wq[0], wq[1])
    k = apply_both(E2.at[1], vr2[0], vr2[1])
    wl = [to_chunk(fold(t[j] + k[j] + wide(e2[1, j]))) for j in range(2)]
    wc = [jnp.where(xi == 0, wl[j], wq[j]) for j in range(2)]
    t = apply_both(D2.at[xi], wc[0], wc[1])
    k = apply_both(E2.at[xi], vc[0], vc[1])
    for j in range(2):
        g.w0[0, j] = fold(t[j] + k[j] + wide(e2[xi, j]))
    t = apply_both(D1.at[1], wc[0], wc[1])
    k = apply_both(E1.at[1], vs[0], vs[1])
    for j in range(2):
        g.w0[1, j] = fold(t[j] + k[j] + wide(e1[1, j]))

    @pl.when(xi == 0)
    def _():
        g.T[0] = D3[m]
        put_product(g.T.at[1], D1.at[1], D2.at[1])

    @pl.when(xi == 1)
    def _():
        g.T[0] = D2[1]
        g.T[1] = D1[1]

    @pl.when(m == 0)
    def _():
        for k in range(2):
            put_product(g.T.at[k], g.T.at[k], D3.at[1])

    def halo_forward():
        mine, theirs, there = halo_pair()
        arrived("halo1", theirs)
        to = jnp.where(h == 0, yup, ydn)
        remote("halo2", theirs, there, (to, s)).start()

    on_chain = (m == 0) & (o > 0) & (o < no - 1)

    @pl.when(jnp.logical_not(on_chain))
    def _():
        halo_forward()

    for j in range(2):

        @pl.when(o < no - 1)
        def _():
            arrived("w%d" % j, win.at[j])

        @pl.when(on_chain)
        def _():
            wout[j] = to_chunk(fold(apply(g.Do, win[j])) + g.beta[j])
            wfar(j).start()

        for k in range(2):
            g.w0[k, j] = g.w0[k, j] + fold(apply(g.T.at[k], win[j]))

    @pl.when(on_chain)
    def _():
        for j in range(2):
            wfar(j).wait_send()
            wnear(j).start()
        halo_forward()

    zs = [pack_columns(g.w0[k, 0], g.w0[k, 1]) for k in range(2)]
    port[e, c] = jnp.where(c == 0, zs[0], zs[1]).astype(BF16)
    g.zout[...] = jnp.where(c == 0, zs[1], zs[0]).astype(BF16)
    mine, slot = port.at[e, c], port.at[e, c]
    for name, to in (("ox", across), ("oup", yup), ("odn", ydn)):
        go(name + "a", mine, slot, (to, s), (name, c))
        go(name + "b", g.zout, slot, (to, s_sib), (name, c))
    go("os", g.zout, slot, sib, ("os", c))

    def half_in(name, f, half):
        ref = port.at[f, half]
        remote("none", ref, ref, sib, (name, half)).wait_recv()
        return ref

    def forward(name, ref, to, recv):
        go(name, ref, ref, (to, s), recv)

    add_step = 16
    n = port.shape[2]

    def add(group, first, last):
        def tile(t, _):
            at = pl.ds(pl.multiple_of(t * add_step, add_step), add_step)
            w = [unpack_halves(port[f, 0, at], port[f, 1, at]) for f in group]
            for j in range(rows):
                if first:
                    re = im = jnp.zeros((add_step, LANES), F32)
                else:
                    re, im = g.acc[j, 0, at], g.acc[j, 1, at]
                for f, (wr, wi) in zip(group, w):
                    k = rows - g.offsets[f] + j
                    gr, gi = ext[k, 0, at].astype(F32), ext[k, 1, at].astype(F32)
                    re += gr * wr - gi * wi
                    im += gr * wi + gi * wr
                if last:
                    g.out[j, 0, 0, at] = re.astype(BF16)
                    g.out[j, 0, 1, at] = im.astype(BF16)
                else:
                    g.acc[j, 0, at], g.acc[j, 1, at] = re, im
            return 0

        lax.fori_loop(0, n // add_step, tile, 0)

    forward("t6", half_in("oup", ydn, 0), yup, "t6")
    forward("t7", half_in("odn", yup, 1), ydn, "t7")
    half_in("oup", ydn, 1)
    half_in("odn", yup, 0)
    for half in range(2):
        ref = half_in("ox", across, half)
        forward("pup%d" % half, ref, yup, ("pup", half))
        forward("pdn%d" % half, ref, ydn, ("pdn", half))
    remote("none", port.at[e, 1 - c], port.at[e, 1 - c], sib, ("os", 1 - c)).wait_recv()

    def screened_tile(t, _):
        at = pl.ds(pl.multiple_of(t * add_step, add_step), add_step)
        re, im = unpack_halves(port[e, 0, at], port[e, 1, at])
        g.screened[0, 0, 0, at] = re.astype(BF16)
        g.screened[0, 0, 1, at] = im.astype(BF16)
        return 0

    lax.fori_loop(0, n // add_step, screened_tile, 0)
    arrived("halo2", ext.at[pl.ds(2 * rows * h, rows)])
    add([e, ydn, yup], True, False)
    opposite = lax.rem(e + 4, ne)
    forward("t8", half_in("pup", across_of(ydn), 0), yup, "t8")
    forward("t9", half_in("pdn", across_of(yup), 1), ydn, "t9")
    arrived("t6", port.at[opposite, 0])
    arrived("t7", port.at[opposite, 1])
    add([across, opposite], False, False)
    half_in("pup", across_of(ydn), 1)
    half_in("pdn", across_of(yup), 0)
    add([across_of(ydn), across_of(yup)], False, False)
    arrived("t8", port.at[across_of(opposite), 0])
    arrived("t9", port.at[across_of(opposite), 1])
    add([across_of(opposite)], False, True)

    for args in sends:
        remote(*args).wait_send()
    for name, ref in (("a2f", A2), ("e2mf", E2), ("d2f", D2)):
        sent(name, ref.at[1 - xi, c], ref.at[1 - xi, c], sib)
    mine, theirs, there = halo_pair()
    sent("halo1", mine, there, (across, s))
    sent("halo2", theirs, there, (across, s))

    @pl.when(m == 0)
    def _():
        sent("b3", b3.at[0], b3.at[0], zup1)
        sent("a3", A3.at[0, c], A3.at[0, c], zup1)
        sent("e3mf", E3.at[1, c], E3.at[1, c], sib)
        sent("d3f", D3.at[1, c], D3.at[1, c], sib)

        @pl.when(o > 0)
        def _():
            for j in range(2):
                wnear(j).wait_send()

    @pl.when(m == 1)
    def _():
        sent("a3f", A3.at[0, c], A3.at[0, c], sib)
        sent("e3m", E3.at[1, c], E3.at[1, c], zdn1)
        sent("d3", D3.at[1, c], D3.at[1, c], zdn1)
        sent("e3", e3.at[1], e3.at[1], zdn1)

        @pl.when((o == 0) | (o < no - 2))
        def _():
            for j in range(2):
                near(vout.at[j], j).wait_send()

        @pl.when((o > 0) & (o == no - 2))
        def _():
            for j in range(2):
                far(vout.at[j], j).wait_send()


def run(nz, ne, lower, pivot, upper, coulomb, greens, offsets):
    n = lower.shape[-1]
    rows = greens.shape[0]
    stack = (2, 2 * n, n)
    chunk = (n, LANES)
    scratch = dict(
        load=pltpu.VMEM((3, 2, n, n), F32),
        cin=pltpu.VMEM((2, n, LANES), F32),
        mst=pltpu.VMEM(stack, BF16),
        bstage=pltpu.VMEM((2,) + chunk, BF16),
        estage=pltpu.VMEM((2,) + chunk, BF16),
        tmp=pltpu.VMEM(stack, BF16),
        Ao=pltpu.VMEM(stack, BF16),
        Do=pltpu.VMEM(stack, BF16),
        Eo=pltpu.VMEM(stack, BF16),
        T=pltpu.VMEM((2,) + stack, BF16),
        w0=pltpu.VMEM((2, 2) + chunk, F32),
        beta=pltpu.VMEM((2,) + chunk, F32),
        zout=pltpu.VMEM(chunk, BF16),
        port=pltpu.VMEM((ne, 2) + chunk, BF16),
        ext=pltpu.VMEM((3 * rows, 2) + chunk, BF16),
        acc=pltpu.VMEM((rows, 2) + chunk, F32),
        load_sem=pltpu.SemaphoreType.DMA((5,)),
        s_sem=pltpu.SemaphoreType.DMA((64,)),
        r_sem=pltpu.SemaphoreType.DMA((64,)),
    )
    for level in "123":
        for name in "ADE":
            scratch[name + level] = pltpu.VMEM((2,) + stack, BF16)
        for name in "be":
            scratch[name + level] = pltpu.VMEM((2, 2) + chunk, BF16)
    for name in ("vin", "vout", "win", "wout"):
        scratch[name] = pltpu.VMEM((2,) + chunk, BF16)
    names = ["offsets", "lower", "pivot", "upper", "coulomb", "greens", "screened", "out"]
    hbm = pl.BlockSpec(memory_space=pltpu.HBM)
    vmem = pl.BlockSpec(memory_space=pltpu.VMEM)
    return pl.pallas_call(
        functools.partial(kernel, nz, names + list(scratch)),
        out_shape=[
            jax.ShapeDtypeStruct(coulomb.shape, BF16),
            jax.ShapeDtypeStruct(greens.shape, BF16),
        ],
        in_specs=[pl.BlockSpec(memory_space=pltpu.SMEM)] + [hbm] * 5,
        out_specs=[vmem] * 2,
        scratch_shapes=list(scratch.values()),
        compiler_params=pltpu.CompilerParams(
            collective_id=0, has_side_effects=True, vmem_limit_bytes=56 * 2**20
        ),
        name="selfenergy",
    )(offsets, lower, pivot, upper, coulomb, greens)


def solution(mesh):
    nz = mesh.shape["slab"] // 4
    ne = mesh.shape["energy"]
    block = P("energy", "slab", None, None, None)
    return jax.shard_map(
        functools.partial(run, nz, ne),
        mesh=mesh,
        in_specs=(block,) * 5 + (P(),),
        out_specs=(block, block),
        check_vma=False,
    )
```

```python
import functools
import types

import jax
import jax.numpy as jnp
from jax import lax
from jax.experimental import pallas as pl
from jax.experimental.pallas import tpu as pltpu
from jax.sharding import PartitionSpec as P

MESH = pl.DeviceIdType.MESH
LANES = 128
BF16 = jnp.bfloat16
F32 = jnp.float32


def dot(a, b):
    return jnp.dot(a, b, preferred_element_type=F32)


def put_stack(ref, part, value):
    n = value.shape[0]
    hi = value.astype(BF16)
    ref[part, 0:n] = hi
    ref[part, n : 2 * n] = (value - hi.astype(F32)).astype(BF16)


def matrix_product(a, b):
    n = a.shape[2]

    def real_product(i, j):
        both = dot(a[i], b[j, 0:n])
        return both[0:n] + both[n : 2 * n] + dot(a[i, 0:n], b[j, n : 2 * n])

    return (
        real_product(0, 0) - real_product(1, 1),
        real_product(0, 1) + real_product(1, 0),
    )


def lane_of(n):
    return lax.broadcasted_iota(jnp.int32, (n, LANES), 1)


def times_i(w):
    f = w.astype(F32)
    group = lane_of(w.shape[0]) // 32
    return jnp.where(group % 2 == 0, -pltpu.roll(f, 96, 1), pltpu.roll(f, 32, 1)).astype(BF16)


def apply(a, w):
    n = a.shape[2]
    r = dot(a[0], w) + dot(a[1], times_i(w))
    return r[0:n] + r[n : 2 * n]


def apply_both(a, w0, w1):
    n = a.shape[2]
    w = jnp.concatenate([w0, w1], axis=1)
    iw = jnp.concatenate([times_i(w0), times_i(w1)], axis=1)
    r = dot(a[0], w) + dot(a[1], iw)
    r = r[0:n] + r[n : 2 * n]
    return r[:, 0:LANES], r[:, LANES : 2 * LANES]


def fold(s):
    return s + pltpu.roll(s, 64, 1)


def to_chunk(v):
    hi = v.astype(BF16).astype(F32)
    return jnp.where(lane_of(v.shape[0]) < 64, hi, v - hi).astype(BF16)


def wide(w):
    return w.astype(F32)


def split_columns(re, im, j):
    lane = lane_of(re.shape[0])
    re = pltpu.roll(re, (LANES - 32 * j) % LANES, 1) if j else re
    im = pltpu.roll(im, (LANES - 32 * j + 32) % LANES, 1)
    pair = jnp.where(lane < 32, re, im)
    return to_chunk(jnp.where(lane < 64, pair, pltpu.roll(pair, 64, 1)))


def put_product(ref, a, b):
    re, im = matrix_product(a, b)
    put_stack(ref, 0, re)
    put_stack(ref, 1, im)


def put_sum(ref, value, stack):
    for part in range(2):
        n = value[part].shape[0]
        put_stack(ref, part, value[part] + wide(stack[part, 0:n]) + wide(stack[part, n : 2 * n]))


def affine_both(a, w, b):
    s = apply_both(a, w[0], w[1])
    return [fold(s[j] + wide(b[j])) for j in range(2)]


def pack_columns(v0, v1):
    lane = lane_of(v0.shape[0])
    low = jnp.where(lane < 32, v0, pltpu.roll(v1, 32, 1))
    high = jnp.where(lane < 96, pltpu.roll(v0, 32, 1), v1)
    return jnp.where(lane < 64, low, high)


def unpack_halves(z0, z1):
    lane = lane_of(z0.shape[0])
    z0, z1 = z0.astype(F32), z1.astype(F32)
    re = jnp.where(lane < 64, z0, pltpu.roll(z1, 64, 1))
    im = jnp.where(lane < 64, pltpu.roll(z0, 64, 1), z1)
    return re, im


def kernel(nz, names, *refs):
    g = types.SimpleNamespace(**dict(zip(names, refs)))
    A1, D1, E1, b1, e1 = g.A1, g.D1, g.E1, g.b1, g.e1
    A2, D2, E2, b2, e2 = g.A2, g.D2, g.E2, g.b2, g.e2
    tmp, vin, vout, win, wout, port, ext = g.tmp, g.vin, g.vout, g.win, g.wout, g.port, g.ext

    e = lax.axis_index("energy")
    s = lax.axis_index("slab")
    ne = lax.axis_size("energy")
    ns = 4 * nz
    no = nz // 2
    rows = g.greens.shape[0]
    c = lax.rem(s, 2)
    q = lax.rem(s // 2, 4)
    xi = lax.rem(q, 2)
    o = s // 8
    early, late = o < no - 1, o == no - 1
    on_chain = (q < 2) & (o > 0) & (o < no - 1)
    h = lax.rem(e, 2)
    s_sib = s + 1 - 2 * c
    sib = (e, s_sib)

    def at(shift):
        return (e, lax.rem(s + shift + ns, ns))

    def across_of(i):
        return i + 1 - 2 * lax.rem(i, 2)

    across = across_of(e)
    yup, ydn = lax.rem(e + 2, ne), lax.rem(e + ne - 2, ne)
    peers = [sib] + [(i, t) for i in (across, yup, ydn) for t in (s, s_sib)]
    chips = [
        (2, 4, 6, 8, -8, -2, -4, -6),
        (-2, 2, 4, 6, 8, -8, -4),
        (2, -2, -4, 4),
        (-2, -4, -6, 8, -8, 2, 4),
    ]

    send_ids, recv_ids = {}, {}
    sends = []
    role_sends = [[], [], [], []]

    def remote(name, src, dst, to, recv=None):
        k = send_ids.setdefault(name, len(send_ids))
        if isinstance(recv, tuple):
            base = recv_ids.setdefault(recv[0] + "0", len(recv_ids))
            recv_ids.setdefault(recv[0] + "1", len(recv_ids))
            r = base + recv[1]
        else:
            r = recv_ids.setdefault(recv or name, len(recv_ids))
        return pltpu.make_async_remote_copy(
            src_ref=src,
            dst_ref=dst,
            send_sem=g.s_sem.at[k],
            recv_sem=g.r_sem.at[r],
            device_id=to,
            device_id_type=MESH,
        )

    def go(*args):
        remote(*args).start()
        sends.append(args)

    def arrived(name, ref):
        remote("none", ref, ref, sib, name).wait_recv()

    def sent(name, ref):
        remote(name, ref, ref, sib, "none").wait_send()

    def send_matrix(role, name, src, dst, to):
        remote(name, src.at[c], getattr(g, dst).at[c], to, (dst, c)).start()
        role_sends[role].append((name, lambda: src.at[c]))

    def send_vector(role, name, src, dst, to):
        remote(name, src, getattr(g, dst), to, dst).start()
        role_sends[role].append((name, lambda: src))

    def first_half(role, dst):
        ref = getattr(g, dst)
        remote("none", ref.at[c], ref.at[c], sib, (dst, c)).wait_recv()
        remote("f" + dst, ref.at[c], ref.at[c], sib, ("f" + dst, c)).start()
        role_sends[role].append(("f" + dst, lambda: ref.at[c]))

    def other_half(dst):
        ref = getattr(g, dst)
        remote("none", ref.at[1 - c], ref.at[1 - c], sib, ("f" + dst, 1 - c)).wait_recv()

    def vector_in(dst):
        arrived(dst, getattr(g, dst))

    def put_vector(ref, values):
        for j in range(2):
            ref[j] = to_chunk(values[j])

    loads = []
    for k, (src, dst) in enumerate(
        [
            (g.lower.at[0, 0], g.load.at[0]),
            (g.coulomb.at[0, 0], g.cin),
            (g.pivot.at[0, 0], g.load.at[1]),
            (g.upper.at[0, 0], g.load.at[2]),
            (g.greens.at[:, 0], ext.at[pl.ds(rows, rows)]),
        ]
    ):
        copy = pltpu.make_async_copy(src, dst, g.load_sem.at[k])
        copy.start()
        loads.append(copy)

    barrier = pltpu.get_barrier_semaphore()
    for to in peers:
        pl.semaphore_signal(barrier, inc=1, device_id=to, device_id_type=MESH)
    for role in range(4):

        @pl.when(q == role)
        def _():
            for shift in chips[role]:
                pl.semaphore_signal(barrier, inc=1, device_id=at(shift), device_id_type=MESH)

    loads[0].wait()
    for part in range(2):
        put_stack(A1.at[c], part, -g.load[0, part])
    loads[1].wait()
    chunks = [split_columns(g.cin[0], g.cin[1], j) for j in range(4)]
    for j in range(2):
        g.bstage[j] = jnp.where(c == 0, chunks[2 + j], chunks[j])
        b1[c, j] = jnp.where(c == 0, chunks[j], chunks[2 + j])
    for role in range(4):

        @pl.when(q == role)
        def _():
            pl.semaphore_wait(barrier, len(peers) + len(chips[role]))

    go("a1", A1.at[c], A1.at[c], sib)
    go("b1", g.bstage, b1.at[c], sib)

    def halo_refs(part):
        half = rows // 2
        mine = ext.at[pl.ds(rows + part * half, half)]
        theirs = ext.at[pl.ds(2 * rows * (1 - h) + part * half, half)]
        there = ext.at[pl.ds(2 * rows * h + part * half, half)]
        return mine, theirs, there

    def halo_start(part=1):
        mine, theirs, there = halo_refs(part)
        remote("halo1%d" % part, mine, there, (across, s)).start()

    def halo_forward(part=1):
        mine, theirs, there = halo_refs(part)
        arrived("halo1%d" % part, theirs)
        to = jnp.where(h == 0, yup, ydn)
        remote("halo2%d" % part, theirs, there, (to, s)).start()

    loads[4].wait()
    halo_start(0)
    loads[3].wait()
    for part in range(2):
        put_stack(D1.at[c], part, -g.load[2, part])
    go("d1", D1.at[c], D1.at[c], sib)
    loads[2].wait()
    for part in range(2):
        put_stack(g.mst, part, g.load[1, part])
    put_product(E1.at[c], g.mst, A1.at[c])
    go("e1m", E1.at[c], E1.at[c], sib)

    arrived("a1", A1.at[1 - c])
    put_product(A2, A1.at[1], A1.at[0])
    for role, dst, shift in ((0, "RA0", 6), (1, "RA1", 4), (2, "RA2", 2)):

        @pl.when(q == role)
        def _():
            send_matrix(role, "a2", A2, dst, at(shift))
            if role == 1:
                send_matrix(role, "a2x", A2, dst, at(-2))

    arrived("b1", b1.at[1 - c])
    put_vector(b2, affine_both(A1.at[1], b1[0], b1[1]))
    for role in (0, 2):

        @pl.when(q == role)
        def _():
            send_vector(role, "b2", b2, "rb", at(2))

    t = apply_both(g.mst, g.bstage[0], g.bstage[1])
    put_vector(g.estage, [fold(v) for v in t])
    go("e1", g.estage, e1.at[c], sib)
    t = apply_both(g.mst, b1[c, 0], b1[c, 1])
    put_vector(e1.at[c], [fold(v) for v in t])
    arrived("e1m", E1.at[1 - c])
    arrived("d1", D1.at[1 - c])
    put_product(tmp, E1.at[1], A1.at[0])
    put_sum(E2, matrix_product(D1.at[0], tmp), E1.at[0])

    @pl.when(q == 1)
    def _():
        send_matrix(1, "e2m", E2, "RE", at(-2))

    @pl.when(q == 3)
    def _():
        send_matrix(3, "e2m", E2, "RE", at(-2))

    put_product(D2, D1.at[0], D1.at[1])

    for role, shift in ((0, 2), (1, -2), (2, 2), (3, -2)):

        @pl.when(q == role)
        def _():
            send_matrix(role, "d2", D2, "RD", at(shift))

    arrived("e1", e1.at[1 - c])

    def merged_e(D0, E_1, e_0, e_1, b_0):
        inner = [to_chunk(v) for v in affine_both(E_1, b_0, e_1)]
        return affine_both(D0, inner, e_0)

    put_vector(e2, merged_e(D1.at[0], E1.at[1], e1[0], e1[1], b1[0]))

    def vout_to(first, j):
        to, name = (at(8), "vfar%d") if first else (at(2), "vnear%d")
        return remote(name % j, vout.at[j], vin.at[j], to, "v%d" % j)

    def wout_to(name, j, shift):
        return remote(name, wout.at[j], win.at[j], at(shift), ("w", j))

    def chain_back(matrix, beta, j):
        remote("none", win.at[j], win.at[j], sib, ("w", j)).wait_recv()
        wout[j] = to_chunk(fold(apply(matrix, win[j]) + beta))
        wout_to("wfar", j, -8).start()

        @pl.when(o > 1)
        def _():
            wout_to("wfar", j, -8).wait_send()

        wout_to("wnear", j, -4).start()
        win_across()

    def win_across():
        remote("wx", win.at[1 - xi], win.at[1 - xi], at(2 - 4 * xi), ("w", 1 - xi)).start()

    halo_forward(0)

    @pl.when(o == 0)
    def _():
        vin[...] = jnp.zeros_like(vin)

    @pl.when(o == no - 1)
    def _():
        win[...] = jnp.zeros_like(win)

    @pl.when(q == 3)
    def _():
        send_vector(3, "e2", e2, "re", at(-2))
        first_half(3, "RA2")
        first_half(3, "RA1")
        vector_in("rb")
        vector_in("bg0")
        other_half("RA2")
        inner = [to_chunk(v) for v in affine_both(g.RA2, g.bg0, g.rb)]
        put_vector(vout, affine_both(A2, inner, b2))

        @pl.when(o == 0)
        def _():
            for j in range(2):
                vout_to(True, j).start()
            for j in range(2):
                vout_to(True, j).wait_send()
                vout_to(False, j).start()

        put_product(g.AG1, A2, g.RA2)
        first_half(3, "RA0")
        other_half("RA1")
        other_half("RA0")
        put_product(g.AG0, g.RA1, g.RA0)
        put_product(g.Ao, g.AG1, g.AG0)

        def last_d():
            first_half(3, "RD")
            other_half("RD")
            put_product(g.G1D, g.RD, D2)
            remote("g1dz", g.G1D.at[c], g.G1D.at[c], at(-4), ("G1D", c)).start()
            halo_start()

        pl.when(o != 1)(last_d)

        @pl.when(o > 0)
        def _():
            for j in range(2):
                arrived("v%d" % j, vin.at[j])

                @pl.when(o < no - 1)
                def _():
                    vout[j] = to_chunk(fold(apply(g.Ao, vin[j]) + wide(vout[j])))

                @pl.when(o < no - 2)
                def _():
                    vout_to(True, j).start()

                @pl.when(o == no - 2)
                def _():
                    vout_to(False, j).start()

            @pl.when(o < no - 2)
            def _():
                for j in range(2):
                    vout_to(True, j).wait_send()
                    vout_to(False, j).start()

            @pl.when(o == no - 2)
            def _():
                for j in range(2):
                    vout_to(False, j).wait_send()
                    vout_to(True, j).start()

        pl.when(o == 1)(last_d)
        role_sends[3].append(("g1dz", lambda: g.G1D.at[c]))
        put_vector(g.v2, affine_both(g.AG0, vin, g.bg0))
        send_vector(3, "v2", g.v2, "v2", at(-2))
        halo_forward()
        put_vector(g.vc, affine_both(g.RA2, g.v2, g.rb))
        g.kap[...] = jnp.zeros_like(g.kap)
        g.T[0] = D2[...]
        g.T[1] = D1[1]

    @pl.when(q == 2)
    def _():
        first_half(2, "RE")
        other_half("RE")
        put_product(tmp, g.RE, A2)
        put_sum(g.G1E, matrix_product(D2, tmp), E2)
        send_matrix(2, "g1e", g.G1E, "G1E", at(-4))
        first_half(2, "RD")
        other_half("RD")
        put_product(g.G1D, D2, g.RD)
        send_matrix(2, "g1d", g.G1D, "G1D", at(-4))
        vector_in("re")
        put_vector(g.eg1, merged_e(D2, g.RE, e2, g.re, b2))
        send_vector(2, "eg1", g.eg1, "eg1", at(-4))
        pl.when(early)(halo_start)
        g.T[0] = g.G1D[...]
        put_product(g.T.at[1], D1.at[1], g.RD)
        pl.when(late)(halo_start)
        halo_forward()
        vector_in("v2")
        g.vc[...] = g.v2[...]
        v3 = [to_chunk(v) for v in affine_both(A2, g.v2, b2)]
        put_vector(g.kap, affine_both(g.RE, v3, g.re))

    @pl.when(q == 1)
    def _():
        send_vector(1, "e2", e2, "re", at(-2))
        vector_in("rb")
        put_vector(g.bg0, affine_both(A2, g.rb, b2))
        send_vector(1, "bg0z", g.bg0, "bg0", at(4))
        send_vector(1, "bg0x", g.bg0, "bg0", at(-2))
        sent("d2", D2.at[c])
        role_sends[1] = [entry for entry in role_sends[1] if entry[0] != "d2"]
        halo_start()
        first_half(1, "RD")
        other_half("RD")
        first_half(1, "G1D")
        other_half("G1D")
        put_product(g.T.at[0], D2, g.G1D)
        put_product(g.Ao, g.RD, g.T.at[0])

        pl.when(o <= 1)(halo_forward)

        @pl.when(on_chain)
        def _():
            vector_in("bt")
            chain_back(g.Ao, wide(g.bt[...]), 0)

        put_product(g.T.at[1], D1.at[1], g.G1D)
        vector_in("v1")
        g.vc[...] = g.v1[...]
        pl.when(o > 1)(halo_forward)
        vector_in("kap")

    @pl.when(q == 0)
    def _():
        first_half(0, "RA1")
        other_half("RA1")
        put_product(g.AG0, g.RA1, A2)
        first_half(0, "RE")
        other_half("RE")
        put_product(tmp, g.RE, A2)
        put_sum(g.EG0, matrix_product(D2, tmp), E2)
        first_half(0, "G1E")
        first_half(0, "RD")
        other_half("G1E")
        put_product(tmp, g.G1E, g.AG0)
        other_half("RD")
        put_product(g.DG0, D2, g.RD)
        put_sum(g.Eo, matrix_product(g.DG0, tmp), g.EG0)
        first_half(0, "G1D")
        pl.when(early)(halo_start)
        other_half("G1D")
        put_product(g.T.at[0], g.DG0, g.G1D)
        vector_in("re")
        eg0 = [to_chunk(v) for v in merged_e(D2, g.RE, e2, g.re, b2)]
        vector_in("bg0")
        pl.when(late)(halo_start)
        vector_in("eg1")
        v = merged_e(g.DG0, g.G1E, eg0, g.eg1, g.bg0)
        for j in range(2):
            g.beta[j] = v[j]

        @pl.when(o > 0)
        def _():
            for j in range(2):
                arrived("v%d" % j, vin.at[j])
                g.beta[j] = g.beta[j] + fold(apply(g.Eo, vin[j]))

                @pl.when(o == no - 1)
                def _():
                    wout[j] = to_chunk(g.beta[j])
                    wout_to("wturn%d" % j, j, -6 - 2 * j).start()

                if j == 0:

                    @pl.when(on_chain)
                    def _():
                        g.bt[...] = to_chunk(g.beta[0])
                        remote("bt", g.bt, g.bt, at(2)).start()

        @pl.when(o == no - 1)
        def _():
            for j in range(2):
                wout_to("wturn%d" % j, j, -6 - 2 * j).wait_send()
                wout_to("wturn%d" % (2 + j), j, -2 - 2 * j).start()

        put_vector(g.v1, affine_both(A2, vin, b2))
        send_vector(0, "v1", g.v1, "v1", at(2))
        pl.when(o <= 1)(halo_forward)

        @pl.when(on_chain)
        def _():
            lanes = lane_of(vin.shape[1])
            chain_back(g.T.at[0], jnp.where(lanes < 64, g.beta[1], 0.0), 1)

        v2 = [to_chunk(v) for v in affine_both(g.AG0, vin, g.bg0)]
        put_vector(g.kap, affine_both(g.G1E, v2, g.eg1))
        send_vector(0, "kap", g.kap, "kap", at(2))
        pl.when(o > 1)(halo_forward)
        put_product(tmp, D1.at[1], g.RD)
        put_product(g.T.at[1], tmp, g.G1D)
        rho = [to_chunk(v) for v in affine_both(g.RE, g.v1, g.re)]
        g.vc[...] = vin[...]
        put_vector(g.k0, affine_both(g.RD, g.kap, rho))

    @pl.when(q != 0)
    def _():
        g.k0[...] = g.kap[...]

    vs = [to_chunk(v) for v in affine_both(A1.at[0], g.vc, b1[0])]
    t = apply_both(D2, g.k0[0], g.k0[1])
    k = apply_both(E2, g.vc[0], g.vc[1])
    for j in range(2):
        g.w0[0, j] = fold(t[j] + k[j] + wide(e2[j]))
    t = apply_both(D1.at[1], g.k0[0], g.k0[1])
    k = apply_both(E1.at[1], vs[0], vs[1])
    for j in range(2):
        g.w0[1, j] = fold(t[j] + k[j] + wide(e1[1, j]))

    @pl.when(early)
    def _():
        @pl.when(jnp.logical_not(on_chain))
        def _():
            remote("none", win.at[1 - xi], win.at[1 - xi], sib, ("w", 1 - xi)).wait_recv()
            win_across()

        for turn in range(2):
            j = 1 - xi if turn == 0 else xi
            if turn == 1:
                remote("none", win.at[j], win.at[j], sib, ("w", j)).wait_recv()
            for k in range(2):
                g.w0[k, j] = g.w0[k, j] + fold(apply(g.T.at[k], win[j]))

    zs = [pack_columns(g.w0[k, 0], g.w0[k, 1]) for k in range(2)]
    port[e, c] = jnp.where(c == 0, zs[0], zs[1]).astype(BF16)
    g.zout[...] = jnp.where(c == 0, zs[1], zs[0]).astype(BF16)
    mine, slot = port.at[e, c], port.at[e, c]
    for name, to in (("ox", across), ("oup", yup), ("odn", ydn)):
        go(name + "a", mine, slot, (to, s), (name, c))
        go(name + "b", g.zout, slot, (to, s_sib), (name, c))
    go("os", g.zout, slot, sib, ("os", c))

    def half_in(name, f, half):
        ref = port.at[f, half]
        remote("none", ref, ref, sib, (name, half)).wait_recv()
        return ref

    def forward(name, ref, to, recv):
        go(name, ref, ref, (to, s), recv)

    add_step = 16
    n = port.shape[2]

    def add(group, first, last):
        def tile(t, _):
            sl = pl.ds(pl.multiple_of(t * add_step, add_step), add_step)
            w = [unpack_halves(port[f, 0, sl], port[f, 1, sl]) for f in group]
            for j in range(rows):
                if first:
                    re = im = jnp.zeros((add_step, LANES), F32)
                else:
                    re, im = g.acc[j, 0, sl], g.acc[j, 1, sl]
                for f, (wr, wi) in zip(group, w):
                    k = rows - g.offsets[f] + j
                    gr, gi = ext[k, 0, sl].astype(F32), ext[k, 1, sl].astype(F32)
                    re += gr * wr - gi * wi
                    im += gr * wi + gi * wr
                if last:
                    g.out[j, 0, 0, sl] = re.astype(BF16)
                    g.out[j, 0, 1, sl] = im.astype(BF16)
                else:
                    g.acc[j, 0, sl], g.acc[j, 1, sl] = re, im
            return 0

        lax.fori_loop(0, n // add_step, tile, 0)

    forward("t6", half_in("oup", ydn, 0), yup, "t6")
    forward("t7", half_in("odn", yup, 1), ydn, "t7")
    half_in("oup", ydn, 1)
    half_in("odn", yup, 0)
    for half in range(2):
        ref = half_in("ox", across, half)
        forward("pup%d" % half, ref, yup, ("pup", half))
        forward("pdn%d" % half, ref, ydn, ("pdn", half))
    remote("none", port.at[e, 1 - c], port.at[e, 1 - c], sib, ("os", 1 - c)).wait_recv()

    def screened_tile(t, _):
        sl = pl.ds(pl.multiple_of(t * add_step, add_step), add_step)
        re, im = unpack_halves(port[e, 0, sl], port[e, 1, sl])
        g.screened[0, 0, 0, sl] = re.astype(BF16)
        g.screened[0, 0, 1, sl] = im.astype(BF16)
        return 0

    lax.fori_loop(0, n // add_step, screened_tile, 0)
    for part in range(2):
        arrived("halo2%d" % part, halo_refs(part)[2])
    add([e, ydn, yup], True, False)
    opposite = lax.rem(e + 4, ne)
    forward("t8", half_in("pup", across_of(ydn), 0), yup, "t8")
    forward("t9", half_in("pdn", across_of(yup), 1), ydn, "t9")
    arrived("t6", port.at[opposite, 0])
    arrived("t7", port.at[opposite, 1])
    add([across, opposite], False, False)
    half_in("pup", across_of(ydn), 1)
    half_in("pdn", across_of(yup), 0)
    add([across_of(ydn), across_of(yup)], False, False)
    arrived("t8", port.at[across_of(opposite), 0])
    arrived("t9", port.at[across_of(opposite), 1])
    add([across_of(opposite)], False, True)

    assert max(len(send_ids), len(recv_ids)) <= g.s_sem.shape[0]

    for args in sends:
        remote(*args).wait_send()
    for part in range(2):
        mine, theirs, there = halo_refs(part)
        sent("halo1%d" % part, mine)
        sent("halo2%d" % part, theirs)
    for role in range(4):

        @pl.when(q == role)
        def _():
            for name, ref in dict(role_sends[role]).items():
                sent(name, ref())

    @pl.when((q == 3) & (o < no - 1))
    def _():
        for j in range(2):

            @pl.when((o > 0) & (o == no - 2))
            def _():
                vout_to(True, j).wait_send()

            @pl.when((o == 0) | (o < no - 2))
            def _():
                vout_to(False, j).wait_send()

    @pl.when(early)
    def _():
        sent("wx", win.at[0])

    @pl.when(on_chain)
    def _():
        @pl.when(o == 1)
        def _():
            sent("wfar", wout.at[0])

        sent("wnear", wout.at[0])

        @pl.when(q == 0)
        def _():
            sent("bt", g.bt)

    @pl.when((q == 0) & late)
    def _():
        for j in range(2):
            sent("wturn%d" % (2 + j), wout.at[0])


def run(nz, ne, lower, pivot, upper, coulomb, greens, offsets):
    n = lower.shape[-1]
    rows = greens.shape[0]
    stack = (2, 2 * n, n)
    chunk = (n, LANES)
    scratch = dict(
        load=pltpu.VMEM((3, 2, n, n), F32),
        cin=pltpu.VMEM((2, n, LANES), F32),
        T=pltpu.VMEM((2,) + stack, BF16),
        w0=pltpu.VMEM((2, 2) + chunk, F32),
        beta=pltpu.VMEM((2,) + chunk, F32),
        zout=pltpu.VMEM(chunk, BF16),
        port=pltpu.VMEM((ne, 2) + chunk, BF16),
        ext=pltpu.VMEM((3 * rows, 2) + chunk, BF16),
        acc=pltpu.VMEM((rows, 2) + chunk, F32),
        load_sem=pltpu.SemaphoreType.DMA((5,)),
        s_sem=pltpu.SemaphoreType.DMA((80,)),
        r_sem=pltpu.SemaphoreType.DMA((80,)),
    )
    for name in ("A1", "D1", "E1"):
        scratch[name] = pltpu.VMEM((2,) + stack, BF16)
    for name in ("b1", "e1"):
        scratch[name] = pltpu.VMEM((2, 2) + chunk, BF16)
    for name in ("mst", "tmp", "A2", "D2", "E2", "RA0", "RA1", "RA2", "RE", "RD", "AG0", "AG1", "EG0", "DG0", "G1E", "G1D", "Ao", "Eo"):
        scratch[name] = pltpu.VMEM(stack, BF16)
    scratch["bt"] = pltpu.VMEM(chunk, BF16)
    for name in ("bstage", "estage", "b2", "e2", "rb", "re", "bg0", "eg1", "v1", "v2", "vc", "kap", "k0", "vin", "vout", "win", "wout"):
        scratch[name] = pltpu.VMEM((2,) + chunk, BF16)
    names = ["offsets", "lower", "pivot", "upper", "coulomb", "greens", "screened", "out"]
    hbm = pl.BlockSpec(memory_space=pltpu.HBM)
    vmem = pl.BlockSpec(memory_space=pltpu.VMEM)
    return pl.pallas_call(
        functools.partial(kernel, nz, names + list(scratch)),
        out_shape=[
            jax.ShapeDtypeStruct(coulomb.shape, BF16),
            jax.ShapeDtypeStruct(greens.shape, BF16),
        ],
        in_specs=[pl.BlockSpec(memory_space=pltpu.SMEM)] + [hbm] * 5,
        out_specs=[vmem] * 2,
        scratch_shapes=list(scratch.values()),
        compiler_params=pltpu.CompilerParams(
            collective_id=0, has_side_effects=True, vmem_limit_bytes=53 * 2**20
        ),
        name="selfenergy",
    )(offsets, lower, pivot, upper, coulomb, greens)


def solution(mesh):
    nz = mesh.shape["slab"] // 4
    ne = mesh.shape["energy"]
    block = P("energy", "slab", None, None, None)
    return jax.shard_map(
        functools.partial(run, nz, ne),
        mesh=mesh,
        in_specs=(block,) * 5 + (P(),),
        out_specs=(block, block),
        check_vma=False,
    )
```

```python
import functools
import types

import jax
import jax.numpy as jnp
from jax import lax
from jax.experimental import pallas as pl
from jax.experimental.pallas import tpu as pltpu
from jax.sharding import PartitionSpec as P

MESH = pl.DeviceIdType.MESH
LANES = 128
BF16 = jnp.bfloat16
F32 = jnp.float32


def dot(a, b):
    return jnp.dot(a, b, preferred_element_type=F32)


def put_stack(ref, part, value):
    n = value.shape[0]
    hi = value.astype(BF16)
    ref[part, 0:n] = hi
    ref[part, n : 2 * n] = (value - hi.astype(F32)).astype(BF16)


def matrix_product(a, b):
    n = a.shape[2]

    def real_product(i, j):
        both = dot(a[i], b[j, 0:n])
        return both[0:n] + both[n : 2 * n] + dot(a[i, 0:n], b[j, n : 2 * n])

    return (
        real_product(0, 0) - real_product(1, 1),
        real_product(0, 1) + real_product(1, 0),
    )


def lane_of(n):
    return lax.broadcasted_iota(jnp.int32, (n, LANES), 1)


def times_i(w):
    f = w.astype(F32)
    group = lane_of(w.shape[0]) // 32
    return jnp.where(group % 2 == 0, -pltpu.roll(f, 96, 1), pltpu.roll(f, 32, 1)).astype(BF16)


def apply(a, w):
    n = a.shape[2]
    r = dot(a[0], w) + dot(a[1], times_i(w))
    return r[0:n] + r[n : 2 * n]


def apply_both(a, w0, w1):
    n = a.shape[2]
    w = jnp.concatenate([w0, w1], axis=1)
    iw = jnp.concatenate([times_i(w0), times_i(w1)], axis=1)
    r = dot(a[0], w) + dot(a[1], iw)
    r = r[0:n] + r[n : 2 * n]
    return r[:, 0:LANES], r[:, LANES : 2 * LANES]


def fold(s):
    return s + pltpu.roll(s, 64, 1)


def to_chunk(v):
    hi = v.astype(BF16).astype(F32)
    return jnp.where(lane_of(v.shape[0]) < 64, hi, v - hi).astype(BF16)


def wide(w):
    return w.astype(F32)


def split_columns(re, im, j):
    lane = lane_of(re.shape[0])
    re = pltpu.roll(re, (LANES - 32 * j) % LANES, 1) if j else re
    im = pltpu.roll(im, (LANES - 32 * j + 32) % LANES, 1)
    pair = jnp.where(lane < 32, re, im)
    return to_chunk(jnp.where(lane < 64, pair, pltpu.roll(pair, 64, 1)))


def put_product(ref, a, b):
    re, im = matrix_product(a, b)
    put_stack(ref, 0, re)
    put_stack(ref, 1, im)


def put_sum(ref, value, stack):
    for part in range(2):
        n = value[part].shape[0]
        put_stack(ref, part, value[part] + wide(stack[part, 0:n]) + wide(stack[part, n : 2 * n]))


def affine_both(a, w, b):
    s = apply_both(a, w[0], w[1])
    return [fold(s[j] + wide(b[j])) for j in range(2)]


def pack_columns(v0, v1):
    lane = lane_of(v0.shape[0])
    low = jnp.where(lane < 32, v0, pltpu.roll(v1, 32, 1))
    high = jnp.where(lane < 96, pltpu.roll(v0, 32, 1), v1)
    return jnp.where(lane < 64, low, high)


def unpack_halves(z0, z1):
    lane = lane_of(z0.shape[0])
    z0, z1 = z0.astype(F32), z1.astype(F32)
    re = jnp.where(lane < 64, z0, pltpu.roll(z1, 64, 1))
    im = jnp.where(lane < 64, pltpu.roll(z0, 64, 1), z1)
    return re, im


def kernel(nz, names, *refs):
    g = types.SimpleNamespace(**dict(zip(names, refs)))
    A1, D1, E1, b1, e1 = g.A1, g.D1, g.E1, g.b1, g.e1
    A2, D2, E2, b2, e2 = g.A2, g.D2, g.E2, g.b2, g.e2
    tmp, vin, vout, win, wout, port, ext = g.tmp, g.vin, g.vout, g.win, g.wout, g.port, g.ext

    e = lax.axis_index("energy")
    s = lax.axis_index("slab")
    ne = lax.axis_size("energy")
    ns = 4 * nz
    no = nz // 2
    rows = g.greens.shape[0]
    c = lax.rem(s, 2)
    q = lax.rem(s // 2, 4)
    xi = lax.rem(q, 2)
    o = s // 8
    early, late = o < no - 1, o == no - 1
    on_chain = (q < 2) & (o > 0) & (o < no - 1)
    h = lax.rem(e, 2)
    s_sib = s + 1 - 2 * c
    sib = (e, s_sib)

    def at(shift):
        return (e, lax.rem(s + shift + ns, ns))

    def across_of(i):
        return i + 1 - 2 * lax.rem(i, 2)

    across = across_of(e)
    yup, ydn = lax.rem(e + 2, ne), lax.rem(e + ne - 2, ne)
    peers = [sib] + [(i, t) for i in (across, yup, ydn) for t in (s, s_sib)]
    chips = [
        (2, 4, 6, 8, -8, -2, -4, -6),
        (-2, 2, 4, 6, 8, -8, -4),
        (2, -2, -4, 4),
        (-2, -4, -6, 8, -8, 2, 4),
    ]

    send_ids, recv_ids = {}, {}
    sends = []
    role_sends = [[], [], [], []]

    def remote(name, src, dst, to, recv=None):
        k = send_ids.setdefault(name, len(send_ids))
        if isinstance(recv, tuple):
            base = recv_ids.setdefault(recv[0] + "0", len(recv_ids))
            recv_ids.setdefault(recv[0] + "1", len(recv_ids))
            r = base + recv[1]
        else:
            r = recv_ids.setdefault(recv or name, len(recv_ids))
        return pltpu.make_async_remote_copy(
            src_ref=src,
            dst_ref=dst,
            send_sem=g.s_sem.at[k],
            recv_sem=g.r_sem.at[r],
            device_id=to,
            device_id_type=MESH,
        )

    def go(*args):
        remote(*args).start()
        sends.append(args)

    def arrived(name, ref):
        remote("none", ref, ref, sib, name).wait_recv()

    def sent(name, ref):
        remote(name, ref, ref, sib, "none").wait_send()

    def send_matrix(role, name, src, dst, to):
        remote(name, src.at[c], getattr(g, dst).at[c], to, (dst, c)).start()
        role_sends[role].append((name, lambda: src.at[c]))

    def send_vector(role, name, src, dst, to):
        remote(name, src, getattr(g, dst), to, dst).start()
        role_sends[role].append((name, lambda: src))

    def first_half(role, dst):
        ref = getattr(g, dst)
        remote("none", ref.at[c], ref.at[c], sib, (dst, c)).wait_recv()
        remote("f" + dst, ref.at[c], ref.at[c], sib, ("f" + dst, c)).start()
        role_sends[role].append(("f" + dst, lambda: ref.at[c]))

    def other_half(dst):
        ref = getattr(g, dst)
        remote("none", ref.at[1 - c], ref.at[1 - c], sib, ("f" + dst, 1 - c)).wait_recv()

    def vector_in(dst):
        arrived(dst, getattr(g, dst))

    def put_vector(ref, values):
        for j in range(2):
            ref[j] = to_chunk(values[j])

    loads = []
    for k, (src, dst) in enumerate(
        [
            (g.lower.at[0, 0], g.load.at[0]),
            (g.coulomb.at[0, 0], g.cin),
            (g.pivot.at[0, 0], g.load.at[1]),
            (g.upper.at[0, 0], g.load.at[2]),
            (g.greens.at[:, 0], ext.at[pl.ds(rows, rows)]),
        ]
    ):
        copy = pltpu.make_async_copy(src, dst, g.load_sem.at[k])
        copy.start()
        loads.append(copy)

    barrier = pltpu.get_barrier_semaphore()
    for to in peers:
        pl.semaphore_signal(barrier, inc=1, device_id=to, device_id_type=MESH)
    for role in range(4):

        @pl.when(q == role)
        def _():
            for shift in chips[role]:
                pl.semaphore_signal(barrier, inc=1, device_id=at(shift), device_id_type=MESH)

    loads[0].wait()
    for part in range(2):
        put_stack(A1.at[c], part, -g.load[0, part])
    loads[1].wait()
    chunks = [split_columns(g.cin[0], g.cin[1], j) for j in range(4)]
    for j in range(2):
        g.bstage[j] = jnp.where(c == 0, chunks[2 + j], chunks[j])
        b1[c, j] = jnp.where(c == 0, chunks[j], chunks[2 + j])
    for role in range(4):

        @pl.when(q == role)
        def _():
            pl.semaphore_wait(barrier, len(peers) + len(chips[role]))

    go("a1", A1.at[c], A1.at[c], sib)
    go("b1", g.bstage, b1.at[c], sib)

    def halo_refs(part):
        half = rows // 2
        mine = ext.at[pl.ds(rows + part * half, half)]
        theirs = ext.at[pl.ds(2 * rows * (1 - h) + part * half, half)]
        there = ext.at[pl.ds(2 * rows * h + part * half, half)]
        return mine, theirs, there

    def halo_start(part=1):
        mine, theirs, there = halo_refs(part)
        remote("halo1%d" % part, mine, there, (across, s)).start()

    def halo_forward(part=1):
        mine, theirs, there = halo_refs(part)
        arrived("halo1%d" % part, theirs)
        to = jnp.where(h == 0, yup, ydn)
        remote("halo2%d" % part, theirs, there, (to, s)).start()

    loads[4].wait()
    halo_start(0)
    loads[3].wait()
    for part in range(2):
        put_stack(D1.at[c], part, -g.load[2, part])
    go("d1", D1.at[c], D1.at[c], sib)
    loads[2].wait()
    for part in range(2):
        put_stack(g.mst, part, g.load[1, part])
    put_product(E1.at[c], g.mst, A1.at[c])
    go("e1m", E1.at[c], E1.at[c], sib)

    arrived("a1", A1.at[1 - c])
    put_product(A2, A1.at[1], A1.at[0])
    for role, dst, shift in ((0, "RA0", 6), (1, "RA1", 4), (2, "RA2", 2)):

        @pl.when(q == role)
        def _():
            send_matrix(role, "a2", A2, dst, at(shift))
            if role == 1:
                send_matrix(role, "a2x", A2, dst, at(-2))

    arrived("b1", b1.at[1 - c])
    put_vector(b2, affine_both(A1.at[1], b1[0], b1[1]))
    for role in (0, 2):

        @pl.when(q == role)
        def _():
            send_vector(role, "b2", b2, "rb", at(2))

    t = apply_both(g.mst, g.bstage[0], g.bstage[1])
    put_vector(g.estage, [fold(v) for v in t])
    go("e1", g.estage, e1.at[c], sib)
    t = apply_both(g.mst, b1[c, 0], b1[c, 1])
    put_vector(e1.at[c], [fold(v) for v in t])
    arrived("e1m", E1.at[1 - c])
    arrived("d1", D1.at[1 - c])
    put_product(tmp, E1.at[1], A1.at[0])
    put_sum(E2, matrix_product(D1.at[0], tmp), E1.at[0])

    @pl.when(q == 1)
    def _():
        send_matrix(1, "e2m", E2, "RE", at(-2))

    @pl.when(q == 3)
    def _():
        send_matrix(3, "e2m", E2, "RE", at(-2))

    put_product(D2, D1.at[0], D1.at[1])

    for role, shift in ((0, 2), (1, -2), (2, 2), (3, -2)):

        @pl.when(q == role)
        def _():
            send_matrix(role, "d2", D2, "RD", at(shift))

    arrived("e1", e1.at[1 - c])

    def merged_e(D0, E_1, e_0, e_1, b_0):
        inner = [to_chunk(v) for v in affine_both(E_1, b_0, e_1)]
        return affine_both(D0, inner, e_0)

    put_vector(e2, merged_e(D1.at[0], E1.at[1], e1[0], e1[1], b1[0]))

    def vout_to(first, j):
        to, name = (at(8), "vfar%d") if first else (at(2), "vnear%d")
        return remote(name % j, vout.at[j], vin.at[j], to, "v%d" % j)

    def wout_to(name, j, shift):
        return remote(name, wout.at[j], win.at[j], at(shift), ("w", j))

    def chain_back(matrix, beta, j):
        remote("none", win.at[j], win.at[j], sib, ("w", j)).wait_recv()
        wout[j] = to_chunk(fold(apply(matrix, win[j]) + beta))
        wout_to("wfar", j, -8).start()

        @pl.when(o > 1)
        def _():
            wout_to("wfar", j, -8).wait_send()

        wout_to("wnear", j, -4).start()
        win_across()

    def win_across():
        remote("wx", win.at[1 - xi], win.at[1 - xi], at(2 - 4 * xi), ("w", 1 - xi)).start()

    halo_forward(0)

    @pl.when(o == 0)
    def _():
        vin[...] = jnp.zeros_like(vin)

    @pl.when(o == no - 1)
    def _():
        win[...] = jnp.zeros_like(win)

    @pl.when(q == 3)
    def _():
        send_vector(3, "e2", e2, "re", at(-2))
        first_half(3, "RA2")
        first_half(3, "RA1")
        vector_in("rb")
        vector_in("bg0")
        other_half("RA2")
        inner = [to_chunk(v) for v in affine_both(g.RA2, g.bg0, g.rb)]
        put_vector(vout, affine_both(A2, inner, b2))

        @pl.when(o == 0)
        def _():
            for j in range(2):
                vout_to(True, j).start()
            for j in range(2):
                vout_to(True, j).wait_send()
                vout_to(False, j).start()

        put_product(g.AG1, A2, g.RA2)
        first_half(3, "RA0")
        other_half("RA1")
        other_half("RA0")
        put_product(g.AG0, g.RA1, g.RA0)
        put_product(g.Ao, g.AG1, g.AG0)

        def last_d():
            first_half(3, "RD")
            other_half("RD")
            put_product(g.G1D, g.RD, D2)
            remote("g1dz", g.G1D.at[c], g.G1D.at[c], at(-4), ("G1D", c)).start()
            halo_start()

        pl.when(o != 1)(last_d)

        @pl.when(o > 0)
        def _():
            for j in range(2):
                arrived("v%d" % j, vin.at[j])

                @pl.when(o < no - 1)
                def _():
                    vout[j] = to_chunk(fold(apply(g.Ao, vin[j]) + wide(vout[j])))

                @pl.when(o < no - 2)
                def _():
                    vout_to(True, j).start()

                @pl.when(o == no - 2)
                def _():
                    vout_to(False, j).start()

            @pl.when(o < no - 2)
            def _():
                for j in range(2):
                    vout_to(True, j).wait_send()
                    vout_to(False, j).start()

            @pl.when(o == no - 2)
            def _():
                for j in range(2):
                    vout_to(False, j).wait_send()
                    vout_to(True, j).start()

        pl.when(o == 1)(last_d)
        role_sends[3].append(("g1dz", lambda: g.G1D.at[c]))
        put_vector(g.v2, affine_both(g.AG0, vin, g.bg0))
        send_vector(3, "v2", g.v2, "v2", at(-2))
        halo_forward()
        put_vector(g.vc, affine_both(g.RA2, g.v2, g.rb))
        g.kap[...] = jnp.zeros_like(g.kap)
        g.T[0] = D2[...]
        g.T[1] = D1[1]

    @pl.when(q == 2)
    def _():
        first_half(2, "RE")
        other_half("RE")
        put_product(tmp, g.RE, A2)
        put_sum(g.G1E, matrix_product(D2, tmp), E2)
        send_matrix(2, "g1e", g.G1E, "G1E", at(-4))
        first_half(2, "RD")
        other_half("RD")
        put_product(g.G1D, D2, g.RD)
        send_matrix(2, "g1d", g.G1D, "G1D", at(-4))
        vector_in("re")
        put_vector(g.eg1, merged_e(D2, g.RE, e2, g.re, b2))
        send_vector(2, "eg1", g.eg1, "eg1", at(-4))
        pl.when(early)(halo_start)
        g.T[0] = g.G1D[...]
        put_product(g.T.at[1], D1.at[1], g.RD)
        pl.when(late)(halo_start)
        halo_forward()
        vector_in("v2")
        g.vc[...] = g.v2[...]
        v3 = [to_chunk(v) for v in affine_both(A2, g.v2, b2)]
        put_vector(g.kap, affine_both(g.RE, v3, g.re))

    @pl.when(q == 1)
    def _():
        send_vector(1, "e2", e2, "re", at(-2))
        vector_in("rb")
        put_vector(g.bg0, affine_both(A2, g.rb, b2))
        send_vector(1, "bg0z", g.bg0, "bg0", at(4))
        send_vector(1, "bg0x", g.bg0, "bg0", at(-2))
        sent("d2", D2.at[c])
        role_sends[1] = [entry for entry in role_sends[1] if entry[0] != "d2"]
        halo_start()
        first_half(1, "RD")
        other_half("RD")
        first_half(1, "G1D")
        other_half("G1D")
        put_product(g.T.at[0], D2, g.G1D)
        put_product(g.Ao, g.RD, g.T.at[0])

        pl.when(o <= 1)(halo_forward)

        @pl.when(on_chain)
        def _():
            vector_in("bt")
            chain_back(g.Ao, wide(g.bt[...]), 0)

        put_product(g.T.at[1], D1.at[1], g.G1D)
        vector_in("v1")
        g.vc[...] = g.v1[...]
        pl.when(o > 1)(halo_forward)
        vector_in("kap")

    @pl.when(q == 0)
    def _():
        first_half(0, "RA1")
        other_half("RA1")
        put_product(g.AG0, g.RA1, A2)
        first_half(0, "RE")
        other_half("RE")
        put_product(tmp, g.RE, A2)
        put_sum(g.EG0, matrix_product(D2, tmp), E2)
        first_half(0, "G1E")
        first_half(0, "RD")
        other_half("G1E")
        put_product(tmp, g.G1E, g.AG0)
        other_half("RD")
        put_product(g.DG0, D2, g.RD)
        put_sum(g.Eo, matrix_product(g.DG0, tmp), g.EG0)
        first_half(0, "G1D")
        pl.when(early)(halo_start)
        other_half("G1D")
        put_product(g.T.at[0], g.DG0, g.G1D)
        vector_in("re")
        eg0 = [to_chunk(v) for v in merged_e(D2, g.RE, e2, g.re, b2)]
        vector_in("bg0")
        pl.when(late)(halo_start)
        vector_in("eg1")
        v = merged_e(g.DG0, g.G1E, eg0, g.eg1, g.bg0)
        for j in range(2):
            g.beta[j] = v[j]

        @pl.when(o > 0)
        def _():
            for j in range(2):
                arrived("v%d" % j, vin.at[j])
                g.beta[j] = g.beta[j] + fold(apply(g.Eo, vin[j]))

                @pl.when(o == no - 1)
                def _():
                    wout[j] = to_chunk(g.beta[j])
                    wout_to("wturn%d" % j, j, -6 - 2 * j).start()

                if j == 0:

                    @pl.when(on_chain)
                    def _():
                        g.bt[...] = to_chunk(g.beta[0])
                        remote("bt", g.bt, g.bt, at(2)).start()

        @pl.when(o == no - 1)
        def _():
            for j in range(2):
                wout_to("wturn%d" % j, j, -6 - 2 * j).wait_send()
                wout_to("wturn%d" % (2 + j), j, -2 - 2 * j).start()

        put_vector(g.v1, affine_both(A2, vin, b2))
        send_vector(0, "v1", g.v1, "v1", at(2))
        pl.when(o <= 1)(halo_forward)

        @pl.when(on_chain)
        def _():
            lanes = lane_of(vin.shape[1])
            chain_back(g.T.at[0], jnp.where(lanes < 64, g.beta[1], 0.0), 1)

        v2 = [to_chunk(v) for v in affine_both(g.AG0, vin, g.bg0)]
        put_vector(g.kap, affine_both(g.G1E, v2, g.eg1))
        send_vector(0, "kap", g.kap, "kap", at(2))
        pl.when(o > 1)(halo_forward)
        put_product(tmp, D1.at[1], g.RD)
        put_product(g.T.at[1], tmp, g.G1D)
        rho = [to_chunk(v) for v in affine_both(g.RE, g.v1, g.re)]
        g.vc[...] = vin[...]
        put_vector(g.k0, affine_both(g.RD, g.kap, rho))

    @pl.when(q != 0)
    def _():
        g.k0[...] = g.kap[...]

    vs = [to_chunk(v) for v in affine_both(A1.at[0], g.vc, b1[0])]
    t = apply_both(D2, g.k0[0], g.k0[1])
    k = apply_both(E2, g.vc[0], g.vc[1])
    for j in range(2):
        g.w0[0, j] = fold(t[j] + k[j] + wide(e2[j]))
    t = apply_both(D1.at[1], g.k0[0], g.k0[1])
    k = apply_both(E1.at[1], vs[0], vs[1])
    for j in range(2):
        g.w0[1, j] = fold(t[j] + k[j] + wide(e1[1, j]))

    @pl.when(early)
    def _():
        @pl.when(jnp.logical_not(on_chain))
        def _():
            remote("none", win.at[1 - xi], win.at[1 - xi], sib, ("w", 1 - xi)).wait_recv()
            win_across()

        for turn in range(2):
            j = 1 - xi if turn == 0 else xi
            if turn == 1:
                remote("none", win.at[j], win.at[j], sib, ("w", j)).wait_recv()
            w = win[j]
            iw = times_i(w)
            n = w.shape[0]
            for k in range(2):
                r = dot(g.T[k, 0], w) + dot(g.T[k, 1], iw)
                g.w0[k, j] = g.w0[k, j] + fold(r[0:n] + r[n : 2 * n])

    zs = [pack_columns(g.w0[k, 0], g.w0[k, 1]) for k in range(2)]
    port[e, c] = jnp.where(c == 0, zs[0], zs[1]).astype(BF16)
    g.zout[...] = jnp.where(c == 0, zs[1], zs[0]).astype(BF16)
    mine, slot = port.at[e, c], port.at[e, c]
    for name, to in (("ox", across), ("oup", yup), ("odn", ydn)):
        go(name + "a", mine, slot, (to, s), (name, c))
        go(name + "b", g.zout, slot, (to, s_sib), (name, c))
    go("os", g.zout, slot, sib, ("os", c))

    def half_in(name, f, half):
        ref = port.at[f, half]
        remote("none", ref, ref, sib, (name, half)).wait_recv()
        return ref

    def forward(name, ref, to, recv):
        go(name, ref, ref, (to, s), recv)

    add_step = 16
    n = port.shape[2]

    def add(group, first, last):
        def tile(t, _):
            sl = pl.ds(pl.multiple_of(t * add_step, add_step), add_step)
            w = [unpack_halves(port[f, 0, sl], port[f, 1, sl]) for f in group]
            for j in range(rows):
                if first:
                    re = im = jnp.zeros((add_step, LANES), F32)
                else:
                    re, im = g.acc[j, 0, sl], g.acc[j, 1, sl]
                for f, (wr, wi) in zip(group, w):
                    k = rows - g.offsets[f] + j
                    gr, gi = ext[k, 0, sl].astype(F32), ext[k, 1, sl].astype(F32)
                    re += gr * wr - gi * wi
                    im += gr * wi + gi * wr
                if last:
                    g.out[j, 0, 0, sl] = re.astype(BF16)
                    g.out[j, 0, 1, sl] = im.astype(BF16)
                else:
                    g.acc[j, 0, sl], g.acc[j, 1, sl] = re, im
            return 0

        lax.fori_loop(0, n // add_step, tile, 0)

    forward("t6", half_in("oup", ydn, 0), yup, "t6")
    forward("t7", half_in("odn", yup, 1), ydn, "t7")
    half_in("oup", ydn, 1)
    half_in("odn", yup, 0)
    for half in range(2):
        ref = half_in("ox", across, half)
        forward("pup%d" % half, ref, yup, ("pup", half))
        forward("pdn%d" % half, ref, ydn, ("pdn", half))
    remote("none", port.at[e, 1 - c], port.at[e, 1 - c], sib, ("os", 1 - c)).wait_recv()

    def screened_tile(t, _):
        sl = pl.ds(pl.multiple_of(t * add_step, add_step), add_step)
        re, im = unpack_halves(port[e, 0, sl], port[e, 1, sl])
        g.screened[0, 0, 0, sl] = re.astype(BF16)
        g.screened[0, 0, 1, sl] = im.astype(BF16)
        return 0

    lax.fori_loop(0, n // add_step, screened_tile, 0)
    for part in range(2):
        arrived("halo2%d" % part, halo_refs(part)[2])
    add([e, ydn, yup], True, False)
    opposite = lax.rem(e + 4, ne)
    forward("t8", half_in("pup", across_of(ydn), 0), yup, "t8")
    forward("t9", half_in("pdn", across_of(yup), 1), ydn, "t9")
    arrived("t6", port.at[opposite, 0])
    arrived("t7", port.at[opposite, 1])
    add([across, opposite], False, False)
    half_in("pup", across_of(ydn), 1)
    half_in("pdn", across_of(yup), 0)
    add([across_of(ydn), across_of(yup)], False, False)
    arrived("t8", port.at[across_of(opposite), 0])
    arrived("t9", port.at[across_of(opposite), 1])
    add([across_of(opposite)], False, True)

    assert max(len(send_ids), len(recv_ids)) <= g.s_sem.shape[0]

    for args in sends:
        remote(*args).wait_send()
    for part in range(2):
        mine, theirs, there = halo_refs(part)
        sent("halo1%d" % part, mine)
        sent("halo2%d" % part, theirs)
    for role in range(4):

        @pl.when(q == role)
        def _():
            for name, ref in dict(role_sends[role]).items():
                sent(name, ref())

    @pl.when((q == 3) & (o < no - 1))
    def _():
        for j in range(2):

            @pl.when((o > 0) & (o == no - 2))
            def _():
                vout_to(True, j).wait_send()

            @pl.when((o == 0) | (o < no - 2))
            def _():
                vout_to(False, j).wait_send()

    @pl.when(early)
    def _():
        sent("wx", win.at[0])

    @pl.when(on_chain)
    def _():
        @pl.when(o == 1)
        def _():
            sent("wfar", wout.at[0])

        sent("wnear", wout.at[0])

        @pl.when(q == 0)
        def _():
            sent("bt", g.bt)

    @pl.when((q == 0) & late)
    def _():
        for j in range(2):
            sent("wturn%d" % (2 + j), wout.at[0])


def run(nz, ne, lower, pivot, upper, coulomb, greens, offsets):
    n = lower.shape[-1]
    rows = greens.shape[0]
    stack = (2, 2 * n, n)
    chunk = (n, LANES)
    scratch = dict(
        load=pltpu.VMEM((3, 2, n, n), F32),
        cin=pltpu.VMEM((2, n, LANES), F32),
        T=pltpu.VMEM((2,) + stack, BF16),
        w0=pltpu.VMEM((2, 2) + chunk, F32),
        beta=pltpu.VMEM((2,) + chunk, F32),
        zout=pltpu.VMEM(chunk, BF16),
        port=pltpu.VMEM((ne, 2) + chunk, BF16),
        ext=pltpu.VMEM((3 * rows, 2) + chunk, BF16),
        acc=pltpu.VMEM((rows, 2) + chunk, F32),
        load_sem=pltpu.SemaphoreType.DMA((5,)),
        s_sem=pltpu.SemaphoreType.DMA((80,)),
        r_sem=pltpu.SemaphoreType.DMA((80,)),
    )
    for name in ("A1", "D1", "E1"):
        scratch[name] = pltpu.VMEM((2,) + stack, BF16)
    for name in ("b1", "e1"):
        scratch[name] = pltpu.VMEM((2, 2) + chunk, BF16)
    for name in ("mst", "tmp", "A2", "D2", "E2", "RA0", "RA1", "RA2", "RE", "RD", "AG0", "AG1", "EG0", "DG0", "G1E", "G1D", "Ao", "Eo"):
        scratch[name] = pltpu.VMEM(stack, BF16)
    scratch["bt"] = pltpu.VMEM(chunk, BF16)
    for name in ("bstage", "estage", "b2", "e2", "rb", "re", "bg0", "eg1", "v1", "v2", "vc", "kap", "k0", "vin", "vout", "win", "wout"):
        scratch[name] = pltpu.VMEM((2,) + chunk, BF16)
    names = ["offsets", "lower", "pivot", "upper", "coulomb", "greens", "screened", "out"]
    hbm = pl.BlockSpec(memory_space=pltpu.HBM)
    vmem = pl.BlockSpec(memory_space=pltpu.VMEM)
    return pl.pallas_call(
        functools.partial(kernel, nz, names + list(scratch)),
        out_shape=[
            jax.ShapeDtypeStruct(coulomb.shape, BF16),
            jax.ShapeDtypeStruct(greens.shape, BF16),
        ],
        in_specs=[pl.BlockSpec(memory_space=pltpu.SMEM)] + [hbm] * 5,
        out_specs=[vmem] * 2,
        scratch_shapes=list(scratch.values()),
        compiler_params=pltpu.CompilerParams(
            collective_id=0, has_side_effects=True, vmem_limit_bytes=53 * 2**20
        ),
        name="selfenergy",
    )(offsets, lower, pivot, upper, coulomb, greens)


def solution(mesh):
    nz = mesh.shape["slab"] // 4
    ne = mesh.shape["energy"]
    block = P("energy", "slab", None, None, None)
    return jax.shard_map(
        functools.partial(run, nz, ne),
        mesh=mesh,
        in_specs=(block,) * 5 + (P(),),
        out_specs=(block, block),
        check_vma=False,
    )
```
